32 devices in a mesh: tm: 4 (over y, x), band: 8 (over z, core).
Axes of the slice: x: 2, y: 2, z: 4, core: 2. Of those that a mesh axis runs over, the one named last changes fastest.
Arguments:
- increments: float32 [4, 4, 2, 1024, 1024], P('tm', None, None, 'band'), may hold values from -6 to 6
- velocity: float32 [4, 2, 1024, 1024], P('tm', None, 'band'), may hold values from -0.4 to 0.4
- diffusivity: float32 [4, 2], replicated, may hold values from 0.03 to 0.22
- scaling: float32 [4, 2, 1024, 1024], P(None, None, 'band'), may hold values from 0.3 to 3
- correlation: float32 [1024, 1024], P('band'), may hold values from -0.2 to 0.5
Outputs:
- weighted_defects: float32 [4, 4, 2, 1024, 1024], P('tm', None, None, 'band')
The draws below stay inside these ranges and needn't reach their ends.
All inputs are finite; a program needn't handle non-finite values.
Results may differ from the reference program's by a relative error of at most 0.000094.
Values sent between devices are 32-bit elements; how exact they have to be, the bound alone decides.
A program may use at most 64 MiB of HBM per device.

```python
import math
import jax
import jax.numpy as jnp
from jax import lax

GRID = 1024
FIELDS = 4
LEVELS = 2
STEPS = 4
WINDOWS = 4


def draw_correlation(key, part):
    index_all = jnp.arange(GRID)
    apart = jnp.abs(index_all[:, None] - index_all[None, :]).astype(jnp.float32)
    first_key, second_key = jax.random.split(jax.random.fold_in(key, 11))
    factor = jax.random.uniform(first_key, (GRID, GRID), jnp.float32, 0.5, 1.5)
    noise = jnp.clip(jax.random.normal(second_key, (GRID, GRID), jnp.float32), -5.0, 5.0) * 0.05
    reach = GRID // 16
    matrix = jnp.eye(GRID, dtype=jnp.float32) + 0.6 * jnp.exp(-apart / reach) * factor + noise
    return 0.2 * matrix


def levels(stream_key, shape, shards, smallest, largest):
    level, own = 1.0, jax.random.fold_in(stream_key, 6)
    for position, blocks in shards:
        heights = jnp.exp(jax.random.uniform(jax.random.fold_in(own, position), (blocks,), jnp.float32, smallest / len(shards), largest / len(shards)))
        level = level * jnp.repeat(heights, shape[position] // blocks).reshape([-1 if axis == position else 1 for axis in range(len(shape))])
    return level


def normal_values(own_key, shape, deviation, bound, shards=(), held_as=jnp.bfloat16):
    values = deviation * jax.random.normal(own_key, shape, jnp.float32)
    if shards:
        values = values * levels(own_key, shape, shards, -0.22, 0.18)
    return jnp.clip(values, -bound, bound).astype(held_as)


def setup_inputs(seed: int = 0) -> dict:
    key_list = jax.random.split(jax.random.key(seed), 6)
    return {
        "increments": normal_values(key_list[0], (WINDOWS, FIELDS, LEVELS, GRID, GRID), 1.0, 6.0, ((0, 4), (3, 8)), jnp.float32),
        "velocity": jnp.clip(jax.random.uniform(key_list[1], (WINDOWS, 2, GRID, GRID), jnp.float32, -0.4, 0.4) * levels(key_list[1], (WINDOWS, 2, GRID, GRID), ((0, 4), (2, 8)), -0.4, 0.0), -0.4, 0.4),
        "diffusivity": jnp.clip(jnp.exp(jax.random.uniform(key_list[2], (FIELDS, LEVELS), jnp.float32, math.log(0.03), math.log(0.22))), 0.03, 0.22),
        "scaling": jnp.clip(jnp.exp(math.log(3.0) - 2.3025851 * jax.random.uniform(key_list[3], (FIELDS, LEVELS, GRID, GRID), jnp.float32) ** levels(key_list[3], (FIELDS, LEVELS, GRID, GRID), ((2, 8),), -0.2, 0.2)), 0.3, 3.0),
        "correlation": draw_correlation(jax.random.fold_in(key_list[5], 71), 0),
    }


def advance(current, east_speed, north_speed, diffuse):
    padded = jnp.pad(current, ((0, 0), (1, 1), (0, 0)))
    upper = padded[:, 2:]
    lower = padded[:, :-2]
    eastern = jnp.roll(current, -1, 2)
    western = jnp.roll(current, 1, 2)
    return (current - 0.5 * east_speed * (eastern - western) - 0.5 * north_speed * (upper - lower)
            + diffuse * (upper + lower + eastern + western - 4.0 * current))


def propagate(initial, speeds, diffuse):
    current = initial
    for section_num in range(STEPS):
        current = advance(current, speeds[0], speeds[1], diffuse)
    return current


def reference(increments, velocity, diffusivity, scaling, correlation):
    channels = FIELDS * LEVELS
    diffuse = diffusivity.reshape(channels, 1, 1)
    sigma = scaling.reshape(channels, GRID, GRID)

    def run_window(pair):
        return propagate(pair[0].reshape(channels, GRID, GRID), pair[1], diffuse)

    ends = lax.map(run_window, (increments, velocity))
    previous = jnp.concatenate([jnp.zeros_like(ends[:1]), ends[:-1]], axis=0)

    def finish(pair):
        defect = pair[0].reshape(channels, GRID, GRID) - pair[1]
        scaled = sigma * defect
        along = jnp.einsum('fyj,ij->fyi', scaled, correlation, precision=lax.Precision.HIGHEST)
        both = jnp.einsum('iy,fyx->fix', correlation, along, precision=lax.Precision.HIGHEST)
        return (sigma * both).reshape(FIELDS, LEVELS, GRID, GRID)

    return lax.map(finish, (increments, previous))
```

```python
import functools
import math

import jax
import jax.numpy as jnp
from jax import lax
from jax.experimental import pallas as pl
from jax.experimental.pallas import tpu as pltpu
from jax.sharding import PartitionSpec as P

FIELDS = 4
LEVELS = 2
STEPS = 4
HALO = 8
LANES = 128
LAG = 2
MESH = pl.DeviceIdType.MESH
VMEM_LIMIT = 52 * 1024 * 1024


def greet(band_size, tm_size, with_tm):
    me = lax.axis_index("band")
    window = lax.axis_index("tm")
    barrier = pltpu.get_barrier_semaphore()
    for d in range(1, band_size):
        pl.semaphore_signal(
            barrier, inc=1, device_id={"band": lax.rem(me + d, band_size)}, device_id_type=MESH
        )
    if with_tm:

        @pl.when(window > 0)
        def _():
            pl.semaphore_signal(barrier, inc=1, device_id={"tm": window - 1}, device_id_type=MESH)

        @pl.when(window < tm_size - 1)
        def _():
            pl.semaphore_signal(barrier, inc=1, device_id={"tm": window + 1}, device_id_type=MESH)

    peers = band_size - 1
    if with_tm:
        peers = peers + (window > 0).astype(jnp.int32) + (window < tm_size - 1).astype(jnp.int32)
    pl.semaphore_wait(barrier, peers)


def spread_kernel(
    band_size, tm_size, group,
    inc, vel, diff, sig,
    recv,
    ends, arrived, scaled, ping, pong, east_speed, north_speed, halo_x, halo_v,
    halo_send, halo_recv, tm_send, tm_recv, a2a_send, a2a_recv, own_sem,
):
    channels, rows, width = inc.shape
    pieces = band_size // group
    piece_width = width // pieces
    steps = channels // group
    me = lax.axis_index("band")
    window = lax.axis_index("tm")

    greet(band_size, tm_size, True)

    def halo_copies(side, neighbour):
        own = pl.ds(0, HALO) if side else pl.ds(rows - HALO, HALO)
        return [
            pltpu.make_async_remote_copy(
                src_ref=array.at[:, own, :],
                dst_ref=store.at[side],
                send_sem=halo_send.at[side, kind],
                recv_sem=halo_recv.at[side, kind],
                device_id={"band": neighbour},
                device_id_type=MESH,
            )
            for kind, (array, store) in enumerate(((vel, halo_v), (inc, halo_x)))
        ]

    @pl.when(me > 0)
    def _():
        for copy in halo_copies(1, me - 1):
            copy.start()

    @pl.when(me < band_size - 1)
    def _():
        for copy in halo_copies(0, me + 1):
            copy.start()

    zeros = jnp.zeros((HALO, width), jnp.float32)
    for store in (ping, pong):
        store[pl.ds(0, HALO), :] = zeros
        store[pl.ds(rows + 3 * HALO, HALO), :] = zeros

    @pl.when(me == 0)
    def _():
        halo_x[0] = jnp.zeros(halo_x.shape[1:], jnp.float32)
        halo_v[0] = jnp.zeros(halo_v.shape[1:], jnp.float32)

    @pl.when(me == band_size - 1)
    def _():
        halo_x[1] = jnp.zeros(halo_x.shape[1:], jnp.float32)
        halo_v[1] = jnp.zeros(halo_v.shape[1:], jnp.float32)

    def inner_speeds(j, carry):
        at = pl.multiple_of(j * HALO, HALO)
        east_speed[pl.ds(at + 2 * HALO, HALO), :] = 0.5 * vel[0, pl.ds(at, HALO), :]
        north_speed[pl.ds(at + 2 * HALO, HALO), :] = 0.5 * vel[1, pl.ds(at, HALO), :]
        return carry

    lax.fori_loop(0, rows // HALO, inner_speeds, 0)

    @pl.when(me > 0)
    def _():
        for copy in halo_copies(0, me - 1):
            copy.wait_recv()

    @pl.when(me < band_size - 1)
    def _():
        for copy in halo_copies(1, me + 1):
            copy.wait_recv()

    for side, at in ((0, HALO), (1, rows + 2 * HALO)):
        east_speed[pl.ds(at, HALO), :] = 0.5 * halo_v[side, 0]
        north_speed[pl.ds(at, HALO), :] = 0.5 * halo_v[side, 1]

    def tangent_step(src, k, first, count, put):
        def strip(j, carry):
            at = pl.multiple_of((first + j) * HALO, HALO)
            near = src[pl.ds(pl.multiple_of(at - HALO, HALO), 3 * HALO), :]
            now = near[HALO : 2 * HALO]
            upper = pltpu.roll(near, 3 * HALO - 1, 0)[HALO : 2 * HALO]
            lower = pltpu.roll(near, 1, 0)[HALO : 2 * HALO]
            eastern = pltpu.roll(now, width - 1, 1)
            western = pltpu.roll(now, 1, 1)
            after = (
                now
                - east_speed[pl.ds(at, HALO), :] * (eastern - western)
                - north_speed[pl.ds(at, HALO), :] * (upper - lower)
                + k * (upper + lower + eastern + western - 4.0 * now)
            )
            place = me * (rows // HALO) + first + j - 2
            inside = (place >= 0) & (place < band_size * (rows // HALO))
            put(at, after * jnp.where(inside, 1.0, 0.0))
            return carry

        lax.fori_loop(0, count, strip, 0)

    def propagate(f):
        k = diff[f]

        def fill(j, carry):
            at = pl.multiple_of(j * HALO, HALO)
            ping[pl.ds(at + 2 * HALO, HALO), :] = inc[f, pl.ds(at, HALO), :]
            return carry

        lax.fori_loop(0, rows // HALO, fill, 0)
        ping[pl.ds(HALO, HALO), :] = halo_x[0, f]
        ping[pl.ds(rows + 2 * HALO, HALO), :] = halo_x[1, f]
        stores = (ping, pong)
        for section in range(STEPS - 1):
            target = stores[(section + 1) % 2]

            def put(at, value, target=target):
                target[pl.ds(at, HALO), :] = value

            tangent_step(stores[section % 2], k, 1, rows // HALO + 2, put)

        def put_end(at, value):
            ends[f, pl.ds(pl.multiple_of(at - 2 * HALO, HALO), HALO), :] = value

        tangent_step(stores[(STEPS - 1) % 2], k, 2, rows // HALO, put_end)

    def tm_copy(f, other):
        return pltpu.make_async_remote_copy(
            src_ref=ends.at[f],
            dst_ref=arrived.at[f],
            send_sem=tm_send.at[f],
            recv_sem=tm_recv.at[f],
            device_id={"tm": other},
            device_id_type=MESH,
        )

    def block_copy(step, block, owner, other):
        return pltpu.make_async_remote_copy(
            src_ref=scaled.at[step, block],
            dst_ref=recv.at[step, pl.ds(pl.multiple_of(owner * rows, rows), rows), :],
            send_sem=a2a_send.at[step, block],
            recv_sem=a2a_recv.at[step, owner],
            device_id={"band": other},
            device_id_type=MESH,
        )

    def own_copy(step):
        return pltpu.make_async_copy(
            scaled.at[step, me],
            recv.at[step, pl.ds(pl.multiple_of(me * rows, rows), rows), :],
            own_sem.at[step],
        )

    def turn(i, carry):
        @pl.when((i < channels) & (window < tm_size - 1))
        def _():
            propagate(i)
            tm_copy(i, window + 1).start()

        @pl.when(i >= LAG)
        def _():
            f = i - LAG
            step, part = f // group, lax.rem(f, group)

            @pl.when(window > 0)
            def _():
                tm_copy(f, window - 1).wait_recv()
                for p in range(pieces):
                    cut = pl.ds(p * piece_width, piece_width)
                    scaled[step, part * pieces + p] = sig[f, :, cut] * (inc[f, :, cut] - arrived[f, :, cut])

            @pl.when(window == 0)
            def _():
                for p in range(pieces):
                    cut = pl.ds(p * piece_width, piece_width)
                    scaled[step, part * pieces + p] = sig[f, :, cut] * inc[f, :, cut]

            for p in range(pieces):
                block = part * pieces + lax.rem(me + p, pieces)

                @pl.when(block != me)
                def _(block=block):
                    block_copy(step, block, me, block).start()

                @pl.when(block == me)
                def _():
                    own_copy(step).start()

        return carry

    lax.fori_loop(0, channels + LAG, turn, 0)

    def finish(step, carry):
        for d in range(1, band_size):
            other = lax.rem(me + d, band_size)
            block_copy(step, other, me, other).wait_send()
            block_copy(step, other, other, other).wait_recv()
        own_copy(step).wait()
        return carry

    lax.fori_loop(0, steps, finish, 0)

    @pl.when(window < tm_size - 1)
    def _():
        def sent(f, carry):
            tm_copy(f, window + 1).wait_send()
            return carry

        lax.fori_loop(0, channels, sent, 0)

    @pl.when(me > 0)
    def _():
        for copy in halo_copies(1, me - 1):
            copy.wait_send()

    @pl.when(me < band_size - 1)
    def _():
        for copy in halo_copies(0, me + 1):
            copy.wait_send()


def halves(value):
    high = value.astype(jnp.bfloat16)
    return high, (value - high.astype(jnp.float32)).astype(jnp.bfloat16)


def correlate_kernel(
    band_size, group,
    blocks, corr, sig,
    out,
    high, low, mixed, back, send_sem, recv_sem,
):
    steps, order, piece_width = blocks.shape
    channels, rows, width = sig.shape
    pieces = band_size // group
    me = lax.axis_index("band")
    tile = min(order, 512)

    greet(band_size, 1, False)

    def split(j, carry):
        at = pl.multiple_of(j * 64, 64)
        high[pl.ds(at, 64), :], low[pl.ds(at, 64), :] = halves(corr[pl.ds(at, 64), :])
        return carry

    lax.fori_loop(0, order // 64, split, 0)

    def block_copy(step, owner, other):
        return pltpu.make_async_remote_copy(
            src_ref=mixed.at[step, pl.ds(pl.multiple_of(other * rows, rows), rows), :],
            dst_ref=back.at[step, owner],
            send_sem=send_sem.at[step, other],
            recv_sem=recv_sem.at[step, owner],
            device_id={"band": other},
            device_id_type=MESH,
        )

    def along_rows(step, carry):
        s_high, s_low = halves(blocks[step])
        both = jnp.concatenate([s_high, s_low], axis=1)

        def row_tile(j, carry):
            at = pl.multiple_of(j * tile, tile)
            one = jnp.dot(high[pl.ds(at, tile), :], both, preferred_element_type=jnp.float32)
            two = jnp.dot(low[pl.ds(at, tile), :], s_high, preferred_element_type=jnp.float32)
            mixed[step, pl.ds(at, tile), :] = one[:, :piece_width] + (one[:, piece_width:] + two)
            return carry

        lax.fori_loop(0, order // tile, row_tile, 0)
        for d in range(1, band_size):
            block_copy(step, me, lax.rem(me + d, band_size)).start()
        back[step, me] = mixed[step, pl.ds(pl.multiple_of(me * rows, rows), rows), :]
        return carry

    lax.fori_loop(0, steps, along_rows, 0)

    contract_last = (((1,), (1,)), ((), ()))

    def along_columns(f, carry):
        step, part = f // group, lax.rem(f, group)
        for p in range(pieces):
            owner = part * pieces + p

            @pl.when(owner != me)
            def _(owner=owner):
                block_copy(step, owner, owner).wait_recv()

        value = jnp.concatenate([back[step, part * pieces + p] for p in range(pieces)], axis=1)
        v_high, v_low = halves(value)
        both = jnp.concatenate([v_high, v_low], axis=0)
        for j in range(width // tile):
            cut = pl.ds(j * tile, tile)
            one = lax.dot_general(both, high[cut, :], contract_last, preferred_element_type=jnp.float32)
            two = lax.dot_general(v_high, low[cut, :], contract_last, preferred_element_type=jnp.float32)
            out[f, :, cut] = sig[f, :, cut] * (one[:rows] + (one[rows:] + two))
        return carry

    lax.fori_loop(0, channels, along_columns, 0)

    def sent(step, carry):
        for d in range(1, band_size):
            block_copy(step, me, lax.rem(me + d, band_size)).wait_send()
        return carry

    lax.fori_loop(0, steps, sent, 0)


def local(increments, velocity, diffusivity, scaling, correlation):
    band_size, tm_size = lax.axis_size("band"), lax.axis_size("tm")
    rows, width = increments.shape[3:]
    channels = FIELDS * LEVELS
    inc = increments.reshape(channels, rows, width)
    sig = scaling.reshape(channels, rows, width)
    diff = diffusivity.reshape(channels)
    group = max(1, LANES * band_size // width)
    steps = channels // group
    piece_width = width * group // band_size
    order = rows * band_size
    dma = pltpu.SemaphoreType.DMA
    f32 = jnp.float32
    vmem = pl.BlockSpec(memory_space=pltpu.VMEM)

    share = math.gcd(rows, tm_size)
    if share == tm_size:
        part = rows // tm_size
        mine = lax.dynamic_slice_in_dim(correlation, lax.axis_index("tm") * part, part, 0)
        corr = lax.all_gather(mine, ("band", "tm"), axis=0, tiled=True)
    else:
        corr = lax.all_gather(correlation, "band", axis=0, tiled=True)

    blocks = pl.pallas_call(
        functools.partial(spread_kernel, band_size, tm_size, group),
        out_shape=jax.ShapeDtypeStruct((steps, order, piece_width), f32),
        in_specs=[vmem, vmem, pl.BlockSpec(memory_space=pltpu.SMEM), vmem],
        out_specs=pl.BlockSpec(memory_space=pl.ANY),
        scratch_shapes=[
            pltpu.VMEM((channels, rows, width), f32),
            pltpu.VMEM((channels, rows, width), f32),
            pltpu.VMEM((steps, band_size, rows, piece_width), f32),
            pltpu.VMEM((rows + 4 * HALO, width), f32),
            pltpu.VMEM((rows + 4 * HALO, width), f32),
            pltpu.VMEM((rows + 4 * HALO, width), f32),
            pltpu.VMEM((rows + 4 * HALO, width), f32),
            pltpu.VMEM((2, channels, HALO, width), f32),
            pltpu.VMEM((2, 2, HALO, width), f32),
            dma((2, 2)),
            dma((2, 2)),
            dma((channels,)),
            dma((channels,)),
            dma((steps, band_size)),
            dma((steps, band_size)),
            dma((steps,)),
        ],
        compiler_params=pltpu.CompilerParams(
            collective_id=0, has_side_effects=True, vmem_limit_bytes=VMEM_LIMIT
        ),
        cost_estimate=pl.CostEstimate(
            flops=200 * channels * rows * width, bytes_accessed=128 * channels * rows * width, transcendentals=0
        ),
        name="spread",
    )(inc, velocity[0], diff, sig)

    out = pl.pallas_call(
        functools.partial(correlate_kernel, band_size, group),
        out_shape=jax.ShapeDtypeStruct((channels, rows, width), f32),
        in_specs=[vmem, vmem, vmem],
        out_specs=vmem,
        scratch_shapes=[
            pltpu.VMEM((order, order), jnp.bfloat16),
            pltpu.VMEM((order, order), jnp.bfloat16),
            pltpu.VMEM((steps, order, piece_width), f32),
            pltpu.VMEM((steps, band_size, rows, piece_width), f32),
            dma((steps, band_size)),
            dma((steps, band_size)),
        ],
        compiler_params=pltpu.CompilerParams(
            collective_id=1, has_side_effects=True, vmem_limit_bytes=VMEM_LIMIT
        ),
        cost_estimate=pl.CostEstimate(
            flops=12 * channels * rows * width * order, bytes_accessed=16 * channels * rows * width, transcendentals=0
        ),
        name="correlate",
    )(blocks, corr, sig)
    return out.reshape(1, FIELDS, LEVELS, rows, width)


def solution(mesh):
    return jax.shard_map(
        local,
        mesh=mesh,
        in_specs=(
            P("tm", None, None, "band", None),
            P("tm", None, "band", None),
            P(),
            P(None, None, "band", None),
            P("band", None),
        ),
        out_specs=P("tm", None, None, "band", None),
        check_vma=False,
    )
```

```python
import functools
import math

import jax
import jax.numpy as jnp
from jax import lax
from jax.experimental import pallas as pl
from jax.experimental.pallas import tpu as pltpu
from jax.sharding import PartitionSpec as P

FIELDS = 4
LEVELS = 2
STEPS = 4
HALO = 8
LANES = 128
LAG = 2
MESH = pl.DeviceIdType.MESH
VMEM_LIMIT = 52 * 1024 * 1024


def greet(band_size, tm_size, with_tm):
    me = lax.axis_index("band")
    window = lax.axis_index("tm")
    barrier = pltpu.get_barrier_semaphore()
    for d in range(1, band_size):
        pl.semaphore_signal(
            barrier, inc=1, device_id={"band": lax.rem(me + d, band_size)}, device_id_type=MESH
        )
    if with_tm:

        @pl.when(window > 0)
        def _():
            pl.semaphore_signal(barrier, inc=1, device_id={"tm": window - 1}, device_id_type=MESH)

        @pl.when(window < tm_size - 1)
        def _():
            pl.semaphore_signal(barrier, inc=1, device_id={"tm": window + 1}, device_id_type=MESH)

    peers = band_size - 1
    if with_tm:
        peers = peers + (window > 0).astype(jnp.int32) + (window < tm_size - 1).astype(jnp.int32)
    pl.semaphore_wait(barrier, peers)


def spread_kernel(
    band_size, tm_size, group,
    inc, vel, diff, sig,
    recv,
    ends, arrived, scaled, ping, pong, east_speed, north_speed, halo_x, halo_v,
    halo_send, halo_recv, tm_send, tm_recv, a2a_send, a2a_recv, own_sem,
):
    channels, rows, width = inc.shape
    pieces = band_size // group
    piece_width = width // pieces
    steps = channels // group
    me = lax.axis_index("band")
    window = lax.axis_index("tm")

    greet(band_size, tm_size, True)

    def halo_copies(side, neighbour):
        own = pl.ds(0, HALO) if side else pl.ds(rows - HALO, HALO)
        return [
            pltpu.make_async_remote_copy(
                src_ref=array.at[:, own, :],
                dst_ref=store.at[side],
                send_sem=halo_send.at[side, kind],
                recv_sem=halo_recv.at[side, kind],
                device_id={"band": neighbour},
                device_id_type=MESH,
            )
            for kind, (array, store) in enumerate(((vel, halo_v), (inc, halo_x)))
        ]

    @pl.when(me > 0)
    def _():
        for copy in halo_copies(1, me - 1):
            copy.start()

    @pl.when(me < band_size - 1)
    def _():
        for copy in halo_copies(0, me + 1):
            copy.start()

    zeros = jnp.zeros((HALO, width), jnp.float32)
    for store in (ping, pong):
        store[pl.ds(0, HALO), :] = zeros
        store[pl.ds(rows + 3 * HALO, HALO), :] = zeros

    @pl.when(me == 0)
    def _():
        halo_x[0] = jnp.zeros(halo_x.shape[1:], jnp.float32)
        halo_v[0] = jnp.zeros(halo_v.shape[1:], jnp.float32)

    @pl.when(me == band_size - 1)
    def _():
        halo_x[1] = jnp.zeros(halo_x.shape[1:], jnp.float32)
        halo_v[1] = jnp.zeros(halo_v.shape[1:], jnp.float32)

    def inner_speeds(j, carry):
        at = pl.multiple_of(j * HALO, HALO)
        east_speed[pl.ds(at + 2 * HALO, HALO), :] = 0.5 * vel[0, pl.ds(at, HALO), :]
        north_speed[pl.ds(at + 2 * HALO, HALO), :] = 0.5 * vel[1, pl.ds(at, HALO), :]
        return carry

    lax.fori_loop(0, rows // HALO, inner_speeds, 0)

    @pl.when(me > 0)
    def _():
        for copy in halo_copies(0, me - 1):
            copy.wait_recv()

    @pl.when(me < band_size - 1)
    def _():
        for copy in halo_copies(1, me + 1):
            copy.wait_recv()

    for side, at in ((0, HALO), (1, rows + 2 * HALO)):
        east_speed[pl.ds(at, HALO), :] = 0.5 * halo_v[side, 0]
        north_speed[pl.ds(at, HALO), :] = 0.5 * halo_v[side, 1]

    def tangent_step(src, k, first, count, put):
        def strip(j, carry):
            at = pl.multiple_of((first + j) * HALO, HALO)
            near = src[pl.ds(pl.multiple_of(at - HALO, HALO), 3 * HALO), :]
            now = near[HALO : 2 * HALO]
            upper = pltpu.roll(near, 3 * HALO - 1, 0)[HALO : 2 * HALO]
            lower = pltpu.roll(near, 1, 0)[HALO : 2 * HALO]
            eastern = pltpu.roll(now, width - 1, 1)
            western = pltpu.roll(now, 1, 1)
            after = (
                now
                - east_speed[pl.ds(at, HALO), :] * (eastern - western)
                - north_speed[pl.ds(at, HALO), :] * (upper - lower)
                + k * (upper + lower + eastern + western - 4.0 * now)
            )
            place = me * (rows // HALO) + first + j - 2
            inside = (place >= 0) & (place < band_size * (rows // HALO))
            put(at, after * jnp.where(inside, 1.0, 0.0))
            return carry

        unroll = max(n for n in range(1, 7) if count % n == 0)
        lax.fori_loop(0, count, strip, 0, unroll=unroll)

    def propagate(f):
        k = diff[f]

        def fill(j, carry):
            at = pl.multiple_of(j * HALO, HALO)
            ping[pl.ds(at + 2 * HALO, HALO), :] = inc[f, pl.ds(at, HALO), :]
            return carry

        lax.fori_loop(0, rows // HALO, fill, 0, unroll=4)
        ping[pl.ds(HALO, HALO), :] = halo_x[0, f]
        ping[pl.ds(rows + 2 * HALO, HALO), :] = halo_x[1, f]
        stores = (ping, pong)
        for section in range(STEPS - 1):
            target = stores[(section + 1) % 2]

            def put(at, value, target=target):
                target[pl.ds(at, HALO), :] = value

            tangent_step(stores[section % 2], k, 1, rows // HALO + 2, put)

        def put_end(at, value):
            ends[f, pl.ds(pl.multiple_of(at - 2 * HALO, HALO), HALO), :] = value

        tangent_step(stores[(STEPS - 1) % 2], k, 2, rows // HALO, put_end)

    def tm_copy(f, other):
        return pltpu.make_async_remote_copy(
            src_ref=ends.at[f],
            dst_ref=arrived.at[f],
            send_sem=tm_send.at[f],
            recv_sem=tm_recv.at[f],
            device_id={"tm": other},
            device_id_type=MESH,
        )

    def block_copy(step, block, owner, other):
        return pltpu.make_async_remote_copy(
            src_ref=scaled.at[step, block],
            dst_ref=recv.at[step, pl.ds(pl.multiple_of(owner * rows, rows), rows), :],
            send_sem=a2a_send.at[step, block],
            recv_sem=a2a_recv.at[step, owner],
            device_id={"band": other},
            device_id_type=MESH,
        )

    def own_copy(step):
        return pltpu.make_async_copy(
            scaled.at[step, me],
            recv.at[step, pl.ds(pl.multiple_of(me * rows, rows), rows), :],
            own_sem.at[step],
        )

    def turn(i, carry):
        @pl.when((i < channels) & (window < tm_size - 1))
        def _():
            propagate(i)
            tm_copy(i, window + 1).start()

        @pl.when(i >= LAG)
        def _():
            f = i - LAG
            step, part = f // group, lax.rem(f, group)

            @pl.when(window > 0)
            def _():
                tm_copy(f, window - 1).wait_recv()
                for p in range(pieces):
                    cut = pl.ds(p * piece_width, piece_width)
                    scaled[step, part * pieces + p] = sig[f, :, cut] * (inc[f, :, cut] - arrived[f, :, cut])

            @pl.when(window == 0)
            def _():
                for p in range(pieces):
                    cut = pl.ds(p * piece_width, piece_width)
                    scaled[step, part * pieces + p] = sig[f, :, cut] * inc[f, :, cut]

            for p in range(pieces):
                block = part * pieces + lax.rem(me + p, pieces)

                @pl.when(block != me)
                def _(block=block):
                    block_copy(step, block, me, block).start()

                @pl.when(block == me)
                def _():
                    own_copy(step).start()

        return carry

    lax.fori_loop(0, channels + LAG, turn, 0)

    def finish(step, carry):
        for d in range(1, band_size):
            other = lax.rem(me + d, band_size)
            block_copy(step, other, me, other).wait_send()
            block_copy(step, other, other, other).wait_recv()
        own_copy(step).wait()
        return carry

    lax.fori_loop(0, steps, finish, 0)

    @pl.when(window < tm_size - 1)
    def _():
        def sent(f, carry):
            tm_copy(f, window + 1).wait_send()
            return carry

        lax.fori_loop(0, channels, sent, 0)

    @pl.when(me > 0)
    def _():
        for copy in halo_copies(1, me - 1):
            copy.wait_send()

    @pl.when(me < band_size - 1)
    def _():
        for copy in halo_copies(0, me + 1):
            copy.wait_send()


def halves(value):
    high = value.astype(jnp.bfloat16)
    return high, (value - high.astype(jnp.float32)).astype(jnp.bfloat16)


def correlate_kernel(
    band_size, group,
    blocks, corr, sig,
    out,
    high, low, mixed, back, send_sem, recv_sem,
):
    steps, order, piece_width = blocks.shape
    channels, rows, width = sig.shape
    pieces = band_size // group
    me = lax.axis_index("band")
    tile = min(order, 512)

    greet(band_size, 1, False)

    def split(j, carry):
        at = pl.multiple_of(j * 64, 64)
        high[pl.ds(at, 64), :], low[pl.ds(at, 64), :] = halves(corr[pl.ds(at, 64), :])
        return carry

    lax.fori_loop(0, order // 64, split, 0)

    def block_copy(step, owner, other):
        return pltpu.make_async_remote_copy(
            src_ref=mixed.at[step, pl.ds(pl.multiple_of(other * rows, rows), rows), :],
            dst_ref=back.at[step, owner],
            send_sem=send_sem.at[step, other],
            recv_sem=recv_sem.at[step, owner],
            device_id={"band": other},
            device_id_type=MESH,
        )

    def along_rows(step, carry):
        s_high, s_low = halves(blocks[step])
        both = jnp.concatenate([s_high, s_low], axis=1)

        def row_tile(j, carry):
            at = pl.multiple_of(j * tile, tile)
            one = jnp.dot(high[pl.ds(at, tile), :], both, preferred_element_type=jnp.float32)
            two = jnp.dot(low[pl.ds(at, tile), :], s_high, preferred_element_type=jnp.float32)
            mixed[step, pl.ds(at, tile), :] = one[:, :piece_width] + (one[:, piece_width:] + two)
            return carry

        lax.fori_loop(0, order // tile, row_tile, 0)
        for d in range(1, band_size):
            block_copy(step, me, lax.rem(me + d, band_size)).start()
        back[step, me] = mixed[step, pl.ds(pl.multiple_of(me * rows, rows), rows), :]
        return carry

    lax.fori_loop(0, steps, along_rows, 0)

    contract_last = (((1,), (1,)), ((), ()))

    def along_columns(f, carry):
        step, part = f // group, lax.rem(f, group)
        for p in range(pieces):
            owner = part * pieces + p

            @pl.when(owner != me)
            def _(owner=owner):
                block_copy(step, owner, owner).wait_recv()

        value = jnp.concatenate([back[step, part * pieces + p] for p in range(pieces)], axis=1)
        v_high, v_low = halves(value)
        both = jnp.concatenate([v_high, v_low], axis=0)
        for j in range(width // tile):
            cut = pl.ds(j * tile, tile)
            one = lax.dot_general(both, high[cut, :], contract_last, preferred_element_type=jnp.float32)
            two = lax.dot_general(v_high, low[cut, :], contract_last, preferred_element_type=jnp.float32)
            out[f, :, cut] = sig[f, :, cut] * (one[:rows] + (one[rows:] + two))
        return carry

    lax.fori_loop(0, channels, along_columns, 0)

    def sent(step, carry):
        for d in range(1, band_size):
            block_copy(step, me, lax.rem(me + d, band_size)).wait_send()
        return carry

    lax.fori_loop(0, steps, sent, 0)


def local(increments, velocity, diffusivity, scaling, correlation):
    band_size, tm_size = lax.axis_size("band"), lax.axis_size("tm")
    rows, width = increments.shape[3:]
    channels = FIELDS * LEVELS
    inc = increments.reshape(channels, rows, width)
    sig = scaling.reshape(channels, rows, width)
    diff = diffusivity.reshape(channels)
    group = max(1, LANES * band_size // width)
    steps = channels // group
    piece_width = width * group // band_size
    order = rows * band_size
    dma = pltpu.SemaphoreType.DMA
    f32 = jnp.float32
    vmem = pl.BlockSpec(memory_space=pltpu.VMEM)

    share = math.gcd(rows, tm_size)
    if share == tm_size:
        part = rows // tm_size
        mine = lax.dynamic_slice_in_dim(correlation, lax.axis_index("tm") * part, part, 0)
        corr = lax.all_gather(mine, ("band", "tm"), axis=0, tiled=True)
    else:
        corr = lax.all_gather(correlation, "band", axis=0, tiled=True)

    blocks = pl.pallas_call(
        functools.partial(spread_kernel, band_size, tm_size, group),
        out_shape=jax.ShapeDtypeStruct((steps, order, piece_width), f32),
        in_specs=[vmem, vmem, pl.BlockSpec(memory_space=pltpu.SMEM), vmem],
        out_specs=pl.BlockSpec(memory_space=pl.ANY),
        scratch_shapes=[
            pltpu.VMEM((channels, rows, width), f32),
            pltpu.VMEM((channels, rows, width), f32),
            pltpu.VMEM((steps, band_size, rows, piece_width), f32),
            pltpu.VMEM((rows + 4 * HALO, width), f32),
            pltpu.VMEM((rows + 4 * HALO, width), f32),
            pltpu.VMEM((rows + 4 * HALO, width), f32),
            pltpu.VMEM((rows + 4 * HALO, width), f32),
            pltpu.VMEM((2, channels, HALO, width), f32),
            pltpu.VMEM((2, 2, HALO, width), f32),
            dma((2, 2)),
            dma((2, 2)),
            dma((channels,)),
            dma((channels,)),
            dma((steps, band_size)),
            dma((steps, band_size)),
            dma((steps,)),
        ],
        compiler_params=pltpu.CompilerParams(
            collective_id=0, has_side_effects=True, vmem_limit_bytes=VMEM_LIMIT
        ),
        cost_estimate=pl.CostEstimate(
            flops=200 * channels * rows * width, bytes_accessed=128 * channels * rows * width, transcendentals=0
        ),
        name="spread",
    )(inc, velocity[0], diff, sig)

    out = pl.pallas_call(
        functools.partial(correlate_kernel, band_size, group),
        out_shape=jax.ShapeDtypeStruct((channels, rows, width), f32),
        in_specs=[vmem, vmem, vmem],
        out_specs=vmem,
        scratch_shapes=[
            pltpu.VMEM((order, order), jnp.bfloat16),
            pltpu.VMEM((order, order), jnp.bfloat16),
            pltpu.VMEM((steps, order, piece_width), f32),
            pltpu.VMEM((steps, band_size, rows, piece_width), f32),
            dma((steps, band_size)),
            dma((steps, band_size)),
        ],
        compiler_params=pltpu.CompilerParams(
            collective_id=1, has_side_effects=True, vmem_limit_bytes=VMEM_LIMIT
        ),
        cost_estimate=pl.CostEstimate(
            flops=12 * channels * rows * width * order, bytes_accessed=16 * channels * rows * width, transcendentals=0
        ),
        name="correlate",
    )(blocks, corr, sig)
    return out.reshape(1, FIELDS, LEVELS, rows, width)


def solution(mesh):
    return jax.shard_map(
        local,
        mesh=mesh,
        in_specs=(
            P("tm", None, None, "band", None),
            P("tm", None, "band", None),
            P(),
            P(None, None, "band", None),
            P("band", None),
        ),
        out_specs=P("tm", None, None, "band", None),
        check_vma=False,
    )
```

```python
import functools

import jax
import jax.numpy as jnp
from jax import lax
from jax.experimental import pallas as pl
from jax.experimental.pallas import tpu as pltpu
from jax.sharding import PartitionSpec as P

FIELDS = 4
LEVELS = 2
STEPS = 4
HALO = 8
LANES = 128
LAG = 2
BACK_LAG = 4
MESH = pl.DeviceIdType.MESH
VMEM_LIMIT = 60 * 1024 * 1024


def greet(band_size, tm_size, sharers):
    me = lax.axis_index("band")
    window = lax.axis_index("tm")
    base = window - lax.rem(window, sharers)
    barrier = pltpu.get_barrier_semaphore()
    for d in range(1, band_size):
        pl.semaphore_signal(
            barrier, inc=1, device_id={"band": lax.rem(me + d, band_size)}, device_id_type=MESH
        )
    for d in range(1, sharers):
        other = base + lax.rem(window - base + d, sharers)
        pl.semaphore_signal(barrier, inc=1, device_id={"tm": other}, device_id_type=MESH)
    before = (window > 0) & (window == base)
    after = (window < tm_size - 1) & (window == base + sharers - 1)

    @pl.when(before)
    def _():
        pl.semaphore_signal(barrier, inc=1, device_id={"tm": window - 1}, device_id_type=MESH)

    @pl.when(after)
    def _():
        pl.semaphore_signal(barrier, inc=1, device_id={"tm": window + 1}, device_id_type=MESH)

    peers = band_size - 1 + sharers - 1 + before.astype(jnp.int32) + after.astype(jnp.int32)
    pl.semaphore_wait(barrier, peers)


def halves(value):
    high = value.astype(jnp.bfloat16)
    return high, (value - high.astype(jnp.float32)).astype(jnp.bfloat16)


def defects_kernel(
    band_size, tm_size, group, sharers,
    inc, vel, diff, sig, corr,
    out,
    full, high, low, mixed, back, recv, ends, arrived, scaled, ping, pong, east_speed, north_speed, halo_x, halo_v,
    halo_send, halo_recv, tm_send, tm_recv, a2a_send, a2a_recv, own_sem, back_send, back_recv,
    share_send, share_recv, window_send, window_recv, core_send, core_recv,
):
    channels, rows, width = inc.shape
    pieces = band_size // group
    piece_width = width // pieces
    steps = channels // group
    me = lax.axis_index("band")
    window = lax.axis_index("tm")

    order = band_size * rows
    part = rows // sharers
    tile = min(order, 512)
    pairs = band_size // 2
    chip, core = me // 2, lax.rem(me, 2)
    sibling = me + 1 - 2 * core
    turn_in = lax.rem(window, sharers)
    base = window - turn_in

    greet(band_size, tm_size, sharers)

    def halo_copies(side, neighbour):
        own = pl.ds(0, HALO) if side else pl.ds(rows - HALO, HALO)
        return [
            pltpu.make_async_remote_copy(
                src_ref=array.at[:, own, :],
                dst_ref=store.at[side],
                send_sem=halo_send.at[side, kind],
                recv_sem=halo_recv.at[side, kind],
                device_id={"band": neighbour},
                device_id_type=MESH,
            )
            for kind, (array, store) in enumerate(((vel, halo_v), (inc, halo_x)))
        ]

    @pl.when(me > 0)
    def _():
        for copy in halo_copies(1, me - 1):
            copy.start()

    @pl.when(me < band_size - 1)
    def _():
        for copy in halo_copies(0, me + 1):
            copy.start()

    def source(h):
        return 2 * lax.rem(chip - h + pairs, pairs) + core

    def share_rows(band, share):
        return pl.ds(pl.multiple_of(band * rows + share * part, part), part)

    def band_rows(band):
        return pl.ds(pl.multiple_of(band * rows, rows), rows)

    def share_copy(h, owner, other):
        return pltpu.make_async_remote_copy(
            src_ref=corr.at[pl.ds(pl.multiple_of(turn_in * part, part), part), :],
            dst_ref=full.at[share_rows(owner, turn_in), :],
            send_sem=share_send.at[h],
            recv_sem=share_recv.at[h],
            device_id={"band": other},
            device_id_type=MESH,
        )

    def window_copy(h, g, share, other):
        at = share_rows(source(h), share)
        return pltpu.make_async_remote_copy(
            src_ref=full.at[at, :],
            dst_ref=full.at[at, :],
            send_sem=window_send.at[h, g],
            recv_sem=window_recv.at[h, g],
            device_id={"tm": other},
            device_id_type=MESH,
        )

    def core_copy(h, owner):
        at = band_rows(owner)
        return pltpu.make_async_remote_copy(
            src_ref=corr if h == 0 else full.at[at, :],
            dst_ref=full.at[at, :],
            send_sem=core_send.at[h],
            recv_sem=core_recv.at[h],
            device_id={"band": sibling},
            device_id_type=MESH,
        )

    def onward(h):
        return 2 * lax.rem(chip + h, pairs) + core

    for h in range(1, pairs):
        share_copy(h, me, onward(h)).start()
    core_copy(0, me).start()

    def pass_to_windows():
        for h in range(1, pairs):
            share_copy(h, source(h), source(h)).wait_recv()
            for g in range(1, sharers):
                window_copy(h, g, turn_in, base + lax.rem(turn_in + g, sharers)).start()

    def pass_to_sibling():
        for h in range(1, pairs):
            for g in range(1, sharers):
                share = lax.rem(turn_in - g + sharers, sharers)
                window_copy(h, g, share, base + share).wait_recv()
            core_copy(h, source(h)).start()

    def split_matrix():
        full[band_rows(me), :] = corr[...]
        for h in range(pairs):
            core_copy(h, source(h) + 1 - 2 * core).wait_recv()

        def split(j, carry):
            at = pl.multiple_of(j * 64, 64)
            high[pl.ds(at, 64), :], low[pl.ds(at, 64), :] = halves(full[pl.ds(at, 64), :])
            return carry

        lax.fori_loop(0, order // 64, split, 0)

    zeros = jnp.zeros((HALO, width), jnp.float32)
    for store in (ping, pong):
        store[pl.ds(0, HALO), :] = zeros
        store[pl.ds(rows + 3 * HALO, HALO), :] = zeros

    @pl.when(me == 0)
    def _():
        halo_x[0] = jnp.zeros(halo_x.shape[1:], jnp.float32)
        halo_v[0] = jnp.zeros(halo_v.shape[1:], jnp.float32)

    @pl.when(me == band_size - 1)
    def _():
        halo_x[1] = jnp.zeros(halo_x.shape[1:], jnp.float32)
        halo_v[1] = jnp.zeros(halo_v.shape[1:], jnp.float32)

    def inner_speeds(j, carry):
        at = pl.multiple_of(j * HALO, HALO)
        east_speed[pl.ds(at + 2 * HALO, HALO), :] = 0.5 * vel[0, pl.ds(at, HALO), :]
        north_speed[pl.ds(at + 2 * HALO, HALO), :] = 0.5 * vel[1, pl.ds(at, HALO), :]
        return carry

    lax.fori_loop(0, rows // HALO, inner_speeds, 0)

    @pl.when(me > 0)
    def _():
        for copy in halo_copies(0, me - 1):
            copy.wait_recv()

    @pl.when(me < band_size - 1)
    def _():
        for copy in halo_copies(1, me + 1):
            copy.wait_recv()

    for side, at in ((0, HALO), (1, rows + 2 * HALO)):
        east_speed[pl.ds(at, HALO), :] = 0.5 * halo_v[side, 0]
        north_speed[pl.ds(at, HALO), :] = 0.5 * halo_v[side, 1]

    def tangent_step(src, k, first, count, put):
        def strip(j, carry):
            at = pl.multiple_of((first + j) * HALO, HALO)
            near = src[pl.ds(pl.multiple_of(at - HALO, HALO), 3 * HALO), :]
            now = near[HALO : 2 * HALO]
            upper = pltpu.roll(near, 3 * HALO - 1, 0)[HALO : 2 * HALO]
            lower = pltpu.roll(near, 1, 0)[HALO : 2 * HALO]
            eastern = pltpu.roll(now, width - 1, 1)
            western = pltpu.roll(now, 1, 1)
            after = (
                now
                - east_speed[pl.ds(at, HALO), :] * (eastern - western)
                - north_speed[pl.ds(at, HALO), :] * (upper - lower)
                + k * (upper + lower + eastern + western - 4.0 * now)
            )
            place = me * (rows // HALO) + first + j - 2
            inside = (place >= 0) & (place < band_size * (rows // HALO))
            put(at, after * jnp.where(inside, 1.0, 0.0))
            return carry

        unroll = max(n for n in range(1, 7) if count % n == 0)
        lax.fori_loop(0, count, strip, 0, unroll=unroll)

    def propagate(f):
        k = diff[f]

        def fill(j, carry):
            at = pl.multiple_of(j * HALO, HALO)
            ping[pl.ds(at + 2 * HALO, HALO), :] = inc[f, pl.ds(at, HALO), :]
            return carry

        lax.fori_loop(0, rows // HALO, fill, 0, unroll=4)
        ping[pl.ds(HALO, HALO), :] = halo_x[0, f]
        ping[pl.ds(rows + 2 * HALO, HALO), :] = halo_x[1, f]
        stores = (ping, pong)
        for section in range(STEPS - 1):
            target = stores[(section + 1) % 2]

            def put(at, value, target=target):
                target[pl.ds(at, HALO), :] = value

            tangent_step(stores[section % 2], k, 1, rows // HALO + 2, put)

        def put_end(at, value):
            ends[f, pl.ds(pl.multiple_of(at - 2 * HALO, HALO), HALO), :] = value

        tangent_step(stores[(STEPS - 1) % 2], k, 2, rows // HALO, put_end)

    def tm_copy(f, other):
        return pltpu.make_async_remote_copy(
            src_ref=ends.at[f],
            dst_ref=arrived.at[f],
            send_sem=tm_send.at[f],
            recv_sem=tm_recv.at[f],
            device_id={"tm": other},
            device_id_type=MESH,
        )

    def block_copy(step, block, owner, other):
        return pltpu.make_async_remote_copy(
            src_ref=scaled.at[step, block],
            dst_ref=recv.at[step, pl.ds(pl.multiple_of(owner * rows, rows), rows), :],
            send_sem=a2a_send.at[step, block],
            recv_sem=a2a_recv.at[step, owner],
            device_id={"band": other},
            device_id_type=MESH,
        )

    def own_copy(step):
        return pltpu.make_async_copy(
            scaled.at[step, me],
            recv.at[step, pl.ds(pl.multiple_of(me * rows, rows), rows), :],
            own_sem.at[step],
        )

    def back_copy(step, owner, other):
        return pltpu.make_async_remote_copy(
            src_ref=mixed.at[step, pl.ds(pl.multiple_of(other * rows, rows), rows), :],
            dst_ref=back.at[step, owner],
            send_sem=back_send.at[step, other],
            recv_sem=back_recv.at[step, owner],
            device_id={"band": other},
            device_id_type=MESH,
        )

    def along_rows(step):
        for d in range(1, band_size):
            other = lax.rem(me + d, band_size)
            block_copy(step, other, other, other).wait_recv()
        own_copy(step).wait()
        s_high, s_low = halves(recv[step])
        both = jnp.concatenate([s_high, s_low], axis=1)

        def row_tile(j, carry):
            at = pl.multiple_of(j * tile, tile)
            one = jnp.dot(high[pl.ds(at, tile), :], both, preferred_element_type=jnp.float32)
            two = jnp.dot(low[pl.ds(at, tile), :], s_high, preferred_element_type=jnp.float32)
            mixed[step, pl.ds(at, tile), :] = one[:, :piece_width] + (one[:, piece_width:] + two)
            return carry

        lax.fori_loop(0, order // tile, row_tile, 0)
        for d in range(1, band_size):
            back_copy(step, me, lax.rem(me + d, band_size)).start()
        back[step, me] = mixed[step, pl.ds(pl.multiple_of(me * rows, rows), rows), :]

    def turn(i, carry):
        @pl.when((i < channels) & (window < tm_size - 1))
        def _():
            propagate(i)
            tm_copy(i, window + 1).start()

        @pl.when((i >= LAG) & (i < channels + LAG))
        def _():
            f = i - LAG
            step, part = f // group, lax.rem(f, group)

            @pl.when(window > 0)
            def _():
                tm_copy(f, window - 1).wait_recv()
                for p in range(pieces):
                    cut = pl.ds(p * piece_width, piece_width)
                    scaled[step, part * pieces + p] = sig[f, :, cut] * (inc[f, :, cut] - arrived[f, :, cut])

            @pl.when(window == 0)
            def _():
                for p in range(pieces):
                    cut = pl.ds(p * piece_width, piece_width)
                    scaled[step, part * pieces + p] = sig[f, :, cut] * inc[f, :, cut]

            for p in range(pieces):
                block = part * pieces + lax.rem(me + p, pieces)

                @pl.when(block != me)
                def _(block=block):
                    block_copy(step, block, me, block).start()

                @pl.when(block == me)
                def _():
                    own_copy(step).start()

        @pl.when(i == 1)
        def _():
            pass_to_windows()

        @pl.when(i == 3)
        def _():
            pass_to_sibling()

        @pl.when(i == BACK_LAG)
        def _():
            split_matrix()

        @pl.when((i >= BACK_LAG) & (lax.rem(i - BACK_LAG + 1, group) == 0))
        def _():
            along_rows((i - BACK_LAG) // group)

        return carry

    lax.fori_loop(0, channels + BACK_LAG, turn, 0)

    contract_last = (((1,), (1,)), ((), ()))

    def along_columns(f, carry):
        step, part = f // group, lax.rem(f, group)
        for p in range(pieces):
            owner = part * pieces + p

            @pl.when(owner != me)
            def _(owner=owner):
                back_copy(step, owner, owner).wait_recv()

        value = jnp.concatenate([back[step, part * pieces + p] for p in range(pieces)], axis=1)
        v_high, v_low = halves(value)
        both = jnp.concatenate([v_high, v_low], axis=0)
        for j in range(width // tile):
            cut = pl.ds(j * tile, tile)
            one = lax.dot_general(both, high[cut, :], contract_last, preferred_element_type=jnp.float32)
            two = lax.dot_general(v_high, low[cut, :], contract_last, preferred_element_type=jnp.float32)
            out[f, :, cut] = sig[f, :, cut] * (one[:rows] + (one[rows:] + two))
        return carry

    lax.fori_loop(0, channels, along_columns, 0)

    def sent(step, carry):
        for d in range(1, band_size):
            back_copy(step, me, lax.rem(me + d, band_size)).wait_send()
        return carry

    lax.fori_loop(0, steps, sent, 0)

    def spread_sent(step, carry):
        for d in range(1, band_size):
            other = lax.rem(me + d, band_size)
            block_copy(step, other, me, other).wait_send()
        return carry

    lax.fori_loop(0, steps, spread_sent, 0)

    for h in range(1, pairs):
        share_copy(h, me, onward(h)).wait_send()
        for g in range(1, sharers):
            window_copy(h, g, turn_in, base + lax.rem(turn_in + g, sharers)).wait_send()
    core_copy(0, me).wait_send()
    for h in range(1, pairs):
        core_copy(h, source(h)).wait_send()

    @pl.when(window < tm_size - 1)
    def _():
        def sent(f, carry):
            tm_copy(f, window + 1).wait_send()
            return carry

        lax.fori_loop(0, channels, sent, 0)

    @pl.when(me > 0)
    def _():
        for copy in halo_copies(1, me - 1):
            copy.wait_send()

    @pl.when(me < band_size - 1)
    def _():
        for copy in halo_copies(0, me + 1):
            copy.wait_send()


def local(increments, velocity, diffusivity, scaling, correlation):
    band_size, tm_size = lax.axis_size("band"), lax.axis_size("tm")
    rows, width = increments.shape[3:]
    channels = FIELDS * LEVELS
    inc = increments.reshape(channels, rows, width)
    sig = scaling.reshape(channels, rows, width)
    diff = diffusivity.reshape(channels)
    group = max(1, LANES * band_size // width)
    steps = channels // group
    piece_width = width * group // band_size
    order = rows * band_size
    dma = pltpu.SemaphoreType.DMA
    f32 = jnp.float32
    vmem = pl.BlockSpec(memory_space=pltpu.VMEM)

    sharers = min(tm_size, rows // HALO)
    while tm_size % sharers or rows % (sharers * HALO):
        sharers -= 1
    pairs = band_size // 2

    out = pl.pallas_call(
        functools.partial(defects_kernel, band_size, tm_size, group, sharers),
        out_shape=jax.ShapeDtypeStruct((channels, rows, width), f32),
        in_specs=[vmem, vmem, pl.BlockSpec(memory_space=pltpu.SMEM), vmem, vmem],
        out_specs=vmem,
        scratch_shapes=[
            pltpu.VMEM((order, order), f32),
            pltpu.VMEM((order, order), jnp.bfloat16),
            pltpu.VMEM((order, order), jnp.bfloat16),
            pltpu.VMEM((steps, order, piece_width), f32),
            pltpu.VMEM((steps, band_size, rows, piece_width), f32),
            pltpu.VMEM((steps, order, piece_width), f32),
            pltpu.VMEM((channels, rows, width), f32),
            pltpu.VMEM((channels, rows, width), f32),
            pltpu.VMEM((steps, band_size, rows, piece_width), f32),
            pltpu.VMEM((rows + 4 * HALO, width), f32),
            pltpu.VMEM((rows + 4 * HALO, width), f32),
            pltpu.VMEM((rows + 4 * HALO, width), f32),
            pltpu.VMEM((rows + 4 * HALO, width), f32),
            pltpu.VMEM((2, channels, HALO, width), f32),
            pltpu.VMEM((2, 2, HALO, width), f32),
            dma((2, 2)),
            dma((2, 2)),
            dma((channels,)),
            dma((channels,)),
            dma((steps, band_size)),
            dma((steps, band_size)),
            dma((steps,)),
            dma((steps, band_size)),
            dma((steps, band_size)),
            dma((pairs,)),
            dma((pairs,)),
            dma((pairs, sharers)),
            dma((pairs, sharers)),
            dma((pairs,)),
            dma((pairs,)),
        ],
        compiler_params=pltpu.CompilerParams(
            collective_id=0, has_side_effects=True, vmem_limit_bytes=VMEM_LIMIT
        ),
        cost_estimate=pl.CostEstimate(
            flops=12 * channels * rows * width * order, bytes_accessed=16 * channels * rows * width, transcendentals=0
        ),
        name="defects",
    )(inc, velocity[0], diff, sig, correlation)
    return out.reshape(1, FIELDS, LEVELS, rows, width)


def solution(mesh):
    return jax.shard_map(
        local,
        mesh=mesh,
        in_specs=(
            P("tm", None, None, "band", None),
            P("tm", None, "band", None),
            P(),
            P(None, None, "band", None),
            P("band", None),
        ),
        out_specs=P("tm", None, None, "band", None),
        check_vma=False,
    )
```

```python
import functools

import jax
import jax.numpy as jnp
from jax import lax
from jax.experimental import pallas as pl
from jax.experimental.pallas import tpu as pltpu
from jax.sharding import PartitionSpec as P

FIELDS = 4
LEVELS = 2
STEPS = 4
HALO = 8
LANES = 128
LAG = 2
BACK_LAG = 4
MESH = pl.DeviceIdType.MESH
VMEM_LIMIT = 60 * 1024 * 1024


def greet(band_size, tm_size, sharers):
    me = lax.axis_index("band")
    window = lax.axis_index("tm")
    base = window - lax.rem(window, sharers)
    barrier = pltpu.get_barrier_semaphore()
    for d in range(1, band_size):
        pl.semaphore_signal(
            barrier, inc=1, device_id={"band": lax.rem(me + d, band_size)}, device_id_type=MESH
        )
    for d in range(1, sharers):
        other = base + lax.rem(window - base + d, sharers)
        pl.semaphore_signal(barrier, inc=1, device_id={"tm": other}, device_id_type=MESH)
    before = (window > 0) & (window == base)
    after = (window < tm_size - 1) & (window == base + sharers - 1)

    @pl.when(before)
    def _():
        pl.semaphore_signal(barrier, inc=1, device_id={"tm": window - 1}, device_id_type=MESH)

    @pl.when(after)
    def _():
        pl.semaphore_signal(barrier, inc=1, device_id={"tm": window + 1}, device_id_type=MESH)

    peers = band_size - 1 + sharers - 1 + before.astype(jnp.int32) + after.astype(jnp.int32)
    pl.semaphore_wait(barrier, peers)


def halves(value):
    high = value.astype(jnp.bfloat16)
    return high, (value - high.astype(jnp.float32)).astype(jnp.bfloat16)


def defects_kernel(
    band_size, tm_size, group, sharers,
    inc_in, vel_in, diff, sig_in, corr,
    result,
    inc, vel, sig, out, vel_load, corr_load, inc_load, sig_load, out_store,
    full, high, low, mixed, back, recv, ends, arrived, scaled, ping, pong, east_speed, north_speed, halo_x, halo_v,
    halo_send, halo_recv, tm_send, tm_recv, a2a_send, a2a_recv, own_sem, back_send, back_recv,
    share_send, share_recv, window_send, window_recv, core_send, core_recv,
):
    channels, rows, width = inc_in.shape
    pieces = band_size // group
    piece_width = width // pieces
    steps = channels // group
    me = lax.axis_index("band")
    window = lax.axis_index("tm")

    order = band_size * rows
    part = rows // sharers
    tile = min(order, 512)
    pairs = band_size // 2
    chip, core = me // 2, lax.rem(me, 2)
    sibling = me + 1 - 2 * core
    turn_in = lax.rem(window, sharers)
    base = window - turn_in

    def inc_copy(f):
        return pltpu.make_async_copy(inc_in.at[f], inc.at[f], inc_load.at[f])

    def sig_copy(f):
        return pltpu.make_async_copy(sig_in.at[f], sig.at[f], sig_load.at[f])

    def out_copy(f):
        return pltpu.make_async_copy(out.at[f], result.at[f], out_store.at[f])

    own_rows = pl.ds(pl.multiple_of(me * rows, rows), rows)
    vel_copy = pltpu.make_async_copy(vel_in, vel, vel_load.at[0])
    corr_copy = pltpu.make_async_copy(corr, full.at[own_rows, :], corr_load.at[0])

    vel_copy.start()

    def load(f, carry):
        inc_copy(f).start()
        return carry

    lax.fori_loop(0, channels, load, 0)

    greet(band_size, tm_size, sharers)

    def halo_copies(side, neighbour):
        own = pl.ds(0, HALO) if side else pl.ds(rows - HALO, HALO)
        return [
            pltpu.make_async_remote_copy(
                src_ref=array.at[:, own, :],
                dst_ref=store.at[side],
                send_sem=halo_send.at[side, kind],
                recv_sem=halo_recv.at[side, kind],
                device_id={"band": neighbour},
                device_id_type=MESH,
            )
            for kind, (array, store) in enumerate(((vel_in, halo_v), (inc_in, halo_x)))
        ]

    @pl.when(me > 0)
    def _():
        for copy in halo_copies(1, me - 1):
            copy.start()

    @pl.when(me < band_size - 1)
    def _():
        for copy in halo_copies(0, me + 1):
            copy.start()

    def source(h):
        return 2 * lax.rem(chip - h + pairs, pairs) + core

    def share_rows(band, share):
        return pl.ds(pl.multiple_of(band * rows + share * part, part), part)

    def band_rows(band):
        return pl.ds(pl.multiple_of(band * rows, rows), rows)

    def share_copy(h, owner, other):
        return pltpu.make_async_remote_copy(
            src_ref=corr.at[pl.ds(pl.multiple_of(turn_in * part, part), part), :],
            dst_ref=full.at[share_rows(owner, turn_in), :],
            send_sem=share_send.at[h],
            recv_sem=share_recv.at[h],
            device_id={"band": other},
            device_id_type=MESH,
        )

    def window_copy(h, g, share, other):
        at = share_rows(source(h), share)
        return pltpu.make_async_remote_copy(
            src_ref=full.at[at, :],
            dst_ref=full.at[at, :],
            send_sem=window_send.at[h, g],
            recv_sem=window_recv.at[h, g],
            device_id={"tm": other},
            device_id_type=MESH,
        )

    def core_copy(h, owner):
        at = band_rows(owner)
        return pltpu.make_async_remote_copy(
            src_ref=corr if h == 0 else full.at[at, :],
            dst_ref=full.at[at, :],
            send_sem=core_send.at[h],
            recv_sem=core_recv.at[h],
            device_id={"band": sibling},
            device_id_type=MESH,
        )

    def onward(h):
        return 2 * lax.rem(chip + h, pairs) + core

    for h in range(1, pairs):
        share_copy(h, me, onward(h)).start()
    core_copy(0, me).start()

    def load_scaling(f, carry):
        sig_copy(f).start()
        return carry

    lax.fori_loop(0, channels, load_scaling, 0)
    corr_copy.start()

    def pass_to_windows():
        for h in range(1, pairs):
            share_copy(h, source(h), source(h)).wait_recv()
            for g in range(1, sharers):
                window_copy(h, g, turn_in, base + lax.rem(turn_in + g, sharers)).start()

    def pass_to_sibling():
        for h in range(1, pairs):
            for g in range(1, sharers):
                share = lax.rem(turn_in - g + sharers, sharers)
                window_copy(h, g, share, base + share).wait_recv()
            core_copy(h, source(h)).start()

    def split_matrix():
        corr_copy.wait()
        for h in range(pairs):
            core_copy(h, source(h) + 1 - 2 * core).wait_recv()

        def split(j, carry):
            at = pl.multiple_of(j * 64, 64)
            high[pl.ds(at, 64), :], low[pl.ds(at, 64), :] = halves(full[pl.ds(at, 64), :])
            return carry

        lax.fori_loop(0, order // 64, split, 0)

    zeros = jnp.zeros((HALO, width), jnp.float32)
    for store in (ping, pong):
        store[pl.ds(0, HALO), :] = zeros
        store[pl.ds(rows + 3 * HALO, HALO), :] = zeros

    @pl.when(me == 0)
    def _():
        halo_x[0] = jnp.zeros(halo_x.shape[1:], jnp.float32)
        halo_v[0] = jnp.zeros(halo_v.shape[1:], jnp.float32)

    @pl.when(me == band_size - 1)
    def _():
        halo_x[1] = jnp.zeros(halo_x.shape[1:], jnp.float32)
        halo_v[1] = jnp.zeros(halo_v.shape[1:], jnp.float32)

    def inner_speeds(j, carry):
        at = pl.multiple_of(j * HALO, HALO)
        east_speed[pl.ds(at + 2 * HALO, HALO), :] = 0.5 * vel[0, pl.ds(at, HALO), :]
        north_speed[pl.ds(at + 2 * HALO, HALO), :] = 0.5 * vel[1, pl.ds(at, HALO), :]
        return carry

    vel_copy.wait()
    lax.fori_loop(0, rows // HALO, inner_speeds, 0, unroll=4)

    @pl.when(me > 0)
    def _():
        for copy in halo_copies(0, me - 1):
            copy.wait_recv()

    @pl.when(me < band_size - 1)
    def _():
        for copy in halo_copies(1, me + 1):
            copy.wait_recv()

    for side, at in ((0, HALO), (1, rows + 2 * HALO)):
        east_speed[pl.ds(at, HALO), :] = 0.5 * halo_v[side, 0]
        north_speed[pl.ds(at, HALO), :] = 0.5 * halo_v[side, 1]

    def tangent_step(src, k, first, count, put):
        def strip(j, carry):
            at = pl.multiple_of((first + j) * HALO, HALO)
            near = src[pl.ds(pl.multiple_of(at - HALO, HALO), 3 * HALO), :]
            now = near[HALO : 2 * HALO]
            upper = pltpu.roll(near, 3 * HALO - 1, 0)[HALO : 2 * HALO]
            lower = pltpu.roll(near, 1, 0)[HALO : 2 * HALO]
            eastern = pltpu.roll(now, width - 1, 1)
            western = pltpu.roll(now, 1, 1)
            after = (
                now
                - east_speed[pl.ds(at, HALO), :] * (eastern - western)
                - north_speed[pl.ds(at, HALO), :] * (upper - lower)
                + k * (upper + lower + eastern + western - 4.0 * now)
            )
            place = me * (rows // HALO) + first + j - 2
            inside = (place >= 0) & (place < band_size * (rows // HALO))
            put(at, after * jnp.where(inside, 1.0, 0.0))
            return carry

        unroll = max(n for n in range(1, 7) if count % n == 0)
        lax.fori_loop(0, count, strip, 0, unroll=unroll)

    def propagate(f):
        k = diff[f]

        def fill(j, carry):
            at = pl.multiple_of(j * HALO, HALO)
            ping[pl.ds(at + 2 * HALO, HALO), :] = inc[f, pl.ds(at, HALO), :]
            return carry

        lax.fori_loop(0, rows // HALO, fill, 0, unroll=4)
        ping[pl.ds(HALO, HALO), :] = halo_x[0, f]
        ping[pl.ds(rows + 2 * HALO, HALO), :] = halo_x[1, f]
        stores = (ping, pong)
        for section in range(STEPS - 1):
            target = stores[(section + 1) % 2]

            def put(at, value, target=target):
                target[pl.ds(at, HALO), :] = value

            tangent_step(stores[section % 2], k, 1, rows // HALO + 2, put)

        def put_end(at, value):
            ends[f, pl.ds(pl.multiple_of(at - 2 * HALO, HALO), HALO), :] = value

        tangent_step(stores[(STEPS - 1) % 2], k, 2, rows // HALO, put_end)

    def tm_copy(f, other):
        return pltpu.make_async_remote_copy(
            src_ref=ends.at[f],
            dst_ref=arrived.at[f],
            send_sem=tm_send.at[f],
            recv_sem=tm_recv.at[f],
            device_id={"tm": other},
            device_id_type=MESH,
        )

    def block_copy(step, block, owner, other):
        return pltpu.make_async_remote_copy(
            src_ref=scaled.at[step, block],
            dst_ref=recv.at[step, pl.ds(pl.multiple_of(owner * rows, rows), rows), :],
            send_sem=a2a_send.at[step, block],
            recv_sem=a2a_recv.at[step, owner],
            device_id={"band": other},
            device_id_type=MESH,
        )

    def own_copy(step):
        return pltpu.make_async_copy(
            scaled.at[step, me],
            recv.at[step, pl.ds(pl.multiple_of(me * rows, rows), rows), :],
            own_sem.at[step],
        )

    def back_copy(step, owner, other):
        return pltpu.make_async_remote_copy(
            src_ref=mixed.at[step, pl.ds(pl.multiple_of(other * rows, rows), rows), :],
            dst_ref=back.at[step, owner],
            send_sem=back_send.at[step, other],
            recv_sem=back_recv.at[step, owner],
            device_id={"band": other},
            device_id_type=MESH,
        )

    def along_rows(step):
        for d in range(1, band_size):
            other = lax.rem(me + d, band_size)
            block_copy(step, other, other, other).wait_recv()
        own_copy(step).wait()
        s_high, s_low = halves(recv[step])
        both = jnp.concatenate([s_high, s_low], axis=1)

        def row_tile(j, carry):
            at = pl.multiple_of(j * tile, tile)
            one = jnp.dot(high[pl.ds(at, tile), :], both, preferred_element_type=jnp.float32)
            two = jnp.dot(low[pl.ds(at, tile), :], s_high, preferred_element_type=jnp.float32)
            mixed[step, pl.ds(at, tile), :] = one[:, :piece_width] + (one[:, piece_width:] + two)
            return carry

        lax.fori_loop(0, order // tile, row_tile, 0)
        for d in range(1, band_size):
            back_copy(step, me, lax.rem(me + d, band_size)).start()
        back[step, me] = mixed[step, pl.ds(pl.multiple_of(me * rows, rows), rows), :]

    def turn(i, carry):
        @pl.when(i < channels)
        def _():
            inc_copy(i).wait()

        @pl.when((i < channels) & (window < tm_size - 1))
        def _():
            propagate(i)
            tm_copy(i, window + 1).start()

        @pl.when((i >= LAG) & (i < channels + LAG))
        def _():
            f = i - LAG
            step, part = f // group, lax.rem(f, group)
            sig_copy(f).wait()

            @pl.when(window > 0)
            def _():
                tm_copy(f, window - 1).wait_recv()
                for p in range(pieces):
                    cut = pl.ds(p * piece_width, piece_width)
                    scaled[step, part * pieces + p] = sig[f, :, cut] * (inc[f, :, cut] - arrived[f, :, cut])

            @pl.when(window == 0)
            def _():
                for p in range(pieces):
                    cut = pl.ds(p * piece_width, piece_width)
                    scaled[step, part * pieces + p] = sig[f, :, cut] * inc[f, :, cut]

            for p in range(pieces):
                block = part * pieces + lax.rem(me + p, pieces)

                @pl.when(block != me)
                def _(block=block):
                    block_copy(step, block, me, block).start()

                @pl.when(block == me)
                def _():
                    own_copy(step).start()

        @pl.when(i == 1)
        def _():
            pass_to_windows()

        @pl.when(i == 3)
        def _():
            pass_to_sibling()

        @pl.when(i == BACK_LAG)
        def _():
            split_matrix()

        @pl.when((i >= BACK_LAG) & (lax.rem(i - BACK_LAG + 1, group) == 0))
        def _():
            along_rows((i - BACK_LAG) // group)

        return carry

    lax.fori_loop(0, channels + BACK_LAG, turn, 0)

    contract_last = (((1,), (1,)), ((), ()))

    def along_columns(f, carry):
        step, part = f // group, lax.rem(f, group)
        for p in range(pieces):
            owner = part * pieces + p

            @pl.when(owner != me)
            def _(owner=owner):
                back_copy(step, owner, owner).wait_recv()

        value = jnp.concatenate([back[step, part * pieces + p] for p in range(pieces)], axis=1)
        v_high, v_low = halves(value)
        both = jnp.concatenate([v_high, v_low], axis=0)
        for j in range(width // tile):
            cut = pl.ds(j * tile, tile)
            one = lax.dot_general(both, high[cut, :], contract_last, preferred_element_type=jnp.float32)
            two = lax.dot_general(v_high, low[cut, :], contract_last, preferred_element_type=jnp.float32)
            out[f, :, cut] = sig[f, :, cut] * (one[:rows] + (one[rows:] + two))
        out_copy(f).start()
        return carry

    lax.fori_loop(0, channels, along_columns, 0)

    def sent(step, carry):
        for d in range(1, band_size):
            back_copy(step, me, lax.rem(me + d, band_size)).wait_send()
        return carry

    lax.fori_loop(0, steps, sent, 0)

    def spread_sent(step, carry):
        for d in range(1, band_size):
            other = lax.rem(me + d, band_size)
            block_copy(step, other, me, other).wait_send()
        return carry

    lax.fori_loop(0, steps, spread_sent, 0)

    for h in range(1, pairs):
        share_copy(h, me, onward(h)).wait_send()
        for g in range(1, sharers):
            window_copy(h, g, turn_in, base + lax.rem(turn_in + g, sharers)).wait_send()
    core_copy(0, me).wait_send()
    for h in range(1, pairs):
        core_copy(h, source(h)).wait_send()

    @pl.when(window < tm_size - 1)
    def _():
        def sent(f, carry):
            tm_copy(f, window + 1).wait_send()
            return carry

        lax.fori_loop(0, channels, sent, 0)

    @pl.when(me > 0)
    def _():
        for copy in halo_copies(1, me - 1):
            copy.wait_send()

    @pl.when(me < band_size - 1)
    def _():
        for copy in halo_copies(0, me + 1):
            copy.wait_send()

    def stored(f, carry):
        out_copy(f).wait()
        return carry

    lax.fori_loop(0, channels, stored, 0)


def local(increments, velocity, diffusivity, scaling, correlation):
    band_size, tm_size = lax.axis_size("band"), lax.axis_size("tm")
    rows, width = increments.shape[3:]
    channels = FIELDS * LEVELS
    inc = increments.reshape(channels, rows, width)
    sig = scaling.reshape(channels, rows, width)
    diff = diffusivity.reshape(channels)
    group = max(1, LANES * band_size // width)
    steps = channels // group
    piece_width = width * group // band_size
    order = rows * band_size
    dma = pltpu.SemaphoreType.DMA
    f32 = jnp.float32
    held = pl.BlockSpec(memory_space=pl.ANY)

    sharers = min(tm_size, rows // HALO)
    while tm_size % sharers or rows % (sharers * HALO):
        sharers -= 1
    pairs = band_size // 2

    out = pl.pallas_call(
        functools.partial(defects_kernel, band_size, tm_size, group, sharers),
        out_shape=jax.ShapeDtypeStruct((channels, rows, width), f32),
        in_specs=[held, held, pl.BlockSpec(memory_space=pltpu.SMEM), held, held],
        out_specs=held,
        scratch_shapes=[
            pltpu.VMEM((channels, rows, width), f32),
            pltpu.VMEM((2, rows, width), f32),
            pltpu.VMEM((channels, rows, width), f32),
            pltpu.VMEM((channels, rows, width), f32),
            dma((1,)),
            dma((1,)),
            dma((channels,)),
            dma((channels,)),
            dma((channels,)),
            pltpu.VMEM((order, order), f32),
            pltpu.VMEM((order, order), jnp.bfloat16),
            pltpu.VMEM((order, order), jnp.bfloat16),
            pltpu.VMEM((steps, order, piece_width), f32),
            pltpu.VMEM((steps, band_size, rows, piece_width), f32),
            pltpu.VMEM((steps, order, piece_width), f32),
            pltpu.VMEM((channels, rows, width), f32),
            pltpu.VMEM((channels, rows, width), f32),
            pltpu.VMEM((steps, band_size, rows, piece_width), f32),
            pltpu.VMEM((rows + 4 * HALO, width), f32),
            pltpu.VMEM((rows + 4 * HALO, width), f32),
            pltpu.VMEM((rows + 4 * HALO, width), f32),
            pltpu.VMEM((rows + 4 * HALO, width), f32),
            pltpu.VMEM((2, channels, HALO, width), f32),
            pltpu.VMEM((2, 2, HALO, width), f32),
            dma((2, 2)),
            dma((2, 2)),
            dma((channels,)),
            dma((channels,)),
            dma((steps, band_size)),
            dma((steps, band_size)),
            dma((steps,)),
            dma((steps, band_size)),
            dma((steps, band_size)),
            dma((pairs,)),
            dma((pairs,)),
            dma((pairs, sharers)),
            dma((pairs, sharers)),
            dma((pairs,)),
            dma((pairs,)),
        ],
        compiler_params=pltpu.CompilerParams(
            collective_id=0, has_side_effects=True, vmem_limit_bytes=VMEM_LIMIT
        ),
        cost_estimate=pl.CostEstimate(
            flops=12 * channels * rows * width * order, bytes_accessed=16 * channels * rows * width, transcendentals=0
        ),
        name="defects",
    )(inc, velocity[0], diff, sig, correlation)
    return out.reshape(1, FIELDS, LEVELS, rows, width)


def solution(mesh):
    return jax.shard_map(
        local,
        mesh=mesh,
        in_specs=(
            P("tm", None, None, "band", None),
            P("tm", None, "band", None),
            P(),
            P(None, None, "band", None),
            P("band", None),
        ),
        out_specs=P("tm", None, None, "band", None),
        check_vma=False,
    )
```

```python
import functools

import jax
import jax.numpy as jnp
from jax import lax
from jax.experimental import pallas as pl
from jax.experimental.pallas import tpu as pltpu
from jax.sharding import PartitionSpec as P

FIELDS = 4
LEVELS = 2
STEPS = 4
HALO = 8
LANES = 128
LAG = 2
BACK_LAG = 5
MESH = pl.DeviceIdType.MESH
VMEM_LIMIT = 60 * 1024 * 1024


def greet(band_size, tm_size, sharers):
    me = lax.axis_index("band")
    window = lax.axis_index("tm")
    base = window - lax.rem(window, sharers)
    barrier = pltpu.get_barrier_semaphore()
    for d in range(1, band_size):
        pl.semaphore_signal(
            barrier, inc=1, device_id={"band": lax.rem(me + d, band_size)}, device_id_type=MESH
        )
    for d in range(1, sharers):
        other = base + lax.rem(window - base + d, sharers)
        pl.semaphore_signal(barrier, inc=1, device_id={"tm": other}, device_id_type=MESH)
    before = (window > 0) & (window == base)
    after = (window < tm_size - 1) & (window == base + sharers - 1)

    @pl.when(before)
    def _():
        pl.semaphore_signal(barrier, inc=1, device_id={"tm": window - 1}, device_id_type=MESH)

    @pl.when(after)
    def _():
        pl.semaphore_signal(barrier, inc=1, device_id={"tm": window + 1}, device_id_type=MESH)

    peers = band_size - 1 + sharers - 1 + before.astype(jnp.int32) + after.astype(jnp.int32)
    pl.semaphore_wait(barrier, peers)


def halves(value):
    high = value.astype(jnp.bfloat16)
    return high, (value - high.astype(jnp.float32)).astype(jnp.bfloat16)


def defects_kernel(
    band_size, tm_size, group, sharers,
    inc_in, vel_in, diff, sig_in, corr,
    result,
    inc, vel, sig, out, vel_load, corr_load, inc_load, sig_load, out_store,
    full, high, low, mixed, back, recv, ends, arrived, scaled, ping, pong, east_speed, north_speed, halo_x, halo_v,
    halo_send, halo_recv, tm_send, tm_recv, a2a_send, a2a_recv, own_sem, back_send, back_recv,
    share_send, share_recv, window_send, window_recv, core_send, core_recv,
):
    channels, rows, width = inc_in.shape
    pieces = band_size // group
    piece_width = width // pieces
    steps = channels // group
    me = lax.axis_index("band")
    window = lax.axis_index("tm")

    order = band_size * rows
    part = rows // sharers
    tile = min(order, 512)
    pairs = band_size // 2
    chip, core = me // 2, lax.rem(me, 2)
    sibling = me + 1 - 2 * core
    turn_in = lax.rem(window, sharers)
    base = window - turn_in

    def inc_copy(f):
        return pltpu.make_async_copy(inc_in.at[f], inc.at[f], inc_load.at[f])

    def sig_copy(f):
        return pltpu.make_async_copy(sig_in.at[f], sig.at[f], sig_load.at[f])

    def out_copy(f):
        return pltpu.make_async_copy(out.at[f], result.at[f], out_store.at[f])

    own_rows = pl.ds(pl.multiple_of(me * rows, rows), rows)
    vel_copy = pltpu.make_async_copy(vel_in, vel, vel_load.at[0])
    corr_copy = pltpu.make_async_copy(corr, full.at[own_rows, :], corr_load.at[0])

    vel_copy.start()

    def load(f, carry):
        inc_copy(f).start()
        return carry

    lax.fori_loop(0, channels, load, 0)

    greet(band_size, tm_size, sharers)

    def halo_copies(side, neighbour):
        own = pl.ds(0, HALO) if side else pl.ds(rows - HALO, HALO)
        return [
            pltpu.make_async_remote_copy(
                src_ref=array.at[:, own, :],
                dst_ref=store.at[side],
                send_sem=halo_send.at[side, kind],
                recv_sem=halo_recv.at[side, kind],
                device_id={"band": neighbour},
                device_id_type=MESH,
            )
            for kind, (array, store) in enumerate(((vel_in, halo_v), (inc_in, halo_x)))
        ]

    @pl.when(me > 0)
    def _():
        for copy in halo_copies(1, me - 1):
            copy.start()

    @pl.when(me < band_size - 1)
    def _():
        for copy in halo_copies(0, me + 1):
            copy.start()

    def source(h):
        return 2 * lax.rem(chip - h + pairs, pairs) + core

    def share_rows(band, share):
        return pl.ds(pl.multiple_of(band * rows + share * part, part), part)

    def band_rows(band):
        return pl.ds(pl.multiple_of(band * rows, rows), rows)

    def share_copy(h, owner, other):
        return pltpu.make_async_remote_copy(
            src_ref=corr.at[pl.ds(pl.multiple_of(turn_in * part, part), part), :],
            dst_ref=full.at[share_rows(owner, turn_in), :],
            send_sem=share_send.at[h],
            recv_sem=share_recv.at[h],
            device_id={"band": other},
            device_id_type=MESH,
        )

    def window_copy(h, g, share, other):
        at = share_rows(source(h), share)
        return pltpu.make_async_remote_copy(
            src_ref=full.at[at, :],
            dst_ref=full.at[at, :],
            send_sem=window_send.at[h, g],
            recv_sem=window_recv.at[h, g],
            device_id={"tm": other},
            device_id_type=MESH,
        )

    def core_copy(h, owner):
        at = band_rows(owner)
        return pltpu.make_async_remote_copy(
            src_ref=corr if h == 0 else full.at[at, :],
            dst_ref=full.at[at, :],
            send_sem=core_send.at[h],
            recv_sem=core_recv.at[h],
            device_id={"band": sibling},
            device_id_type=MESH,
        )

    def onward(h):
        return 2 * lax.rem(chip + h, pairs) + core

    for h in range(1, pairs):
        share_copy(h, me, onward(h)).start()
    core_copy(0, me).start()

    def load_scaling(f, carry):
        sig_copy(f).start()
        return carry

    lax.fori_loop(0, channels, load_scaling, 0)
    corr_copy.start()

    def pass_to_windows():
        for h in range(1, pairs):
            share_copy(h, source(h), source(h)).wait_recv()
            for g in range(1, sharers):
                window_copy(h, g, turn_in, base + lax.rem(turn_in + g, sharers)).start()

    def pass_to_sibling():
        for h in range(1, pairs):
            for g in range(1, sharers):
                share = lax.rem(turn_in - g + sharers, sharers)
                window_copy(h, g, share, base + share).wait_recv()
            core_copy(h, source(h)).start()

    def split_matrix():
        corr_copy.wait()
        for h in range(pairs):
            core_copy(h, source(h) + 1 - 2 * core).wait_recv()

        def split(j, carry):
            at = pl.multiple_of(j * 64, 64)
            high[pl.ds(at, 64), :], low[pl.ds(at, 64), :] = halves(full[pl.ds(at, 64), :])
            return carry

        lax.fori_loop(0, order // 64, split, 0)

    zeros = jnp.zeros((HALO, width), jnp.float32)
    for store in (ping, pong):
        store[pl.ds(0, HALO), :] = zeros
        store[pl.ds(rows + 3 * HALO, HALO), :] = zeros

    @pl.when(me == 0)
    def _():
        halo_x[0] = jnp.zeros(halo_x.shape[1:], jnp.float32)
        halo_v[0] = jnp.zeros(halo_v.shape[1:], jnp.float32)

    @pl.when(me == band_size - 1)
    def _():
        halo_x[1] = jnp.zeros(halo_x.shape[1:], jnp.float32)
        halo_v[1] = jnp.zeros(halo_v.shape[1:], jnp.float32)

    def inner_speeds(j, carry):
        at = pl.multiple_of(j * HALO, HALO)
        east_speed[pl.ds(at + 2 * HALO, HALO), :] = 0.5 * vel[0, pl.ds(at, HALO), :]
        north_speed[pl.ds(at + 2 * HALO, HALO), :] = 0.5 * vel[1, pl.ds(at, HALO), :]
        return carry

    vel_copy.wait()
    lax.fori_loop(0, rows // HALO, inner_speeds, 0, unroll=4)

    @pl.when(me > 0)
    def _():
        for copy in halo_copies(0, me - 1):
            copy.wait_recv()

    @pl.when(me < band_size - 1)
    def _():
        for copy in halo_copies(1, me + 1):
            copy.wait_recv()

    for side, at in ((0, HALO), (1, rows + 2 * HALO)):
        east_speed[pl.ds(at, HALO), :] = 0.5 * halo_v[side, 0]
        north_speed[pl.ds(at, HALO), :] = 0.5 * halo_v[side, 1]

    def tangent_step(src, k, first, count, put):
        def strip(j, carry):
            at = pl.multiple_of((first + j) * HALO, HALO)
            near = src[pl.ds(pl.multiple_of(at - HALO, HALO), 3 * HALO), :]
            now = near[HALO : 2 * HALO]
            upper = pltpu.roll(near, 3 * HALO - 1, 0)[HALO : 2 * HALO]
            lower = pltpu.roll(near, 1, 0)[HALO : 2 * HALO]
            eastern = pltpu.roll(now, width - 1, 1)
            western = pltpu.roll(now, 1, 1)
            after = (
                now
                - east_speed[pl.ds(at, HALO), :] * (eastern - western)
                - north_speed[pl.ds(at, HALO), :] * (upper - lower)
                + k * (upper + lower + eastern + western - 4.0 * now)
            )
            place = me * (rows // HALO) + first + j - 2
            inside = (place >= 0) & (place < band_size * (rows // HALO))
            put(at, after * jnp.where(inside, 1.0, 0.0))
            return carry

        unroll = max(n for n in range(1, 7) if count % n == 0)
        lax.fori_loop(0, count, strip, 0, unroll=unroll)

    def propagate(f):
        k = diff[f]

        def fill(j, carry):
            at = pl.multiple_of(j * HALO, HALO)
            ping[pl.ds(at + 2 * HALO, HALO), :] = inc[f, pl.ds(at, HALO), :]
            return carry

        lax.fori_loop(0, rows // HALO, fill, 0, unroll=4)
        ping[pl.ds(HALO, HALO), :] = halo_x[0, f]
        ping[pl.ds(rows + 2 * HALO, HALO), :] = halo_x[1, f]
        stores = (ping, pong)
        for section in range(STEPS - 1):
            target = stores[(section + 1) % 2]

            def put(at, value, target=target):
                target[pl.ds(at, HALO), :] = value

            tangent_step(stores[section % 2], k, 1, rows // HALO + 2, put)

        def put_end(at, value):
            ends[f, pl.ds(pl.multiple_of(at - 2 * HALO, HALO), HALO), :] = value

        tangent_step(stores[(STEPS - 1) % 2], k, 2, rows // HALO, put_end)

    def tm_copy(f, other):
        return pltpu.make_async_remote_copy(
            src_ref=ends.at[f],
            dst_ref=arrived.at[f],
            send_sem=tm_send.at[f],
            recv_sem=tm_recv.at[f],
            device_id={"tm": other},
            device_id_type=MESH,
        )

    def block_copy(step, block, owner, other):
        return pltpu.make_async_remote_copy(
            src_ref=scaled.at[step, block],
            dst_ref=recv.at[step, pl.ds(pl.multiple_of(owner * rows, rows), rows), :],
            send_sem=a2a_send.at[step, block],
            recv_sem=a2a_recv.at[step, owner],
            device_id={"band": other},
            device_id_type=MESH,
        )

    def own_copy(step):
        return pltpu.make_async_copy(
            scaled.at[step, me],
            recv.at[step, pl.ds(pl.multiple_of(me * rows, rows), rows), :],
            own_sem.at[step],
        )

    def back_copy(step, owner, other):
        return pltpu.make_async_remote_copy(
            src_ref=mixed.at[step, pl.ds(pl.multiple_of(other * rows, rows), rows), :],
            dst_ref=back.at[step, owner],
            send_sem=back_send.at[step, other],
            recv_sem=back_recv.at[step, owner],
            device_id={"band": other},
            device_id_type=MESH,
        )

    def along_rows(step):
        for d in range(1, band_size):
            other = lax.rem(me + d, band_size)
            block_copy(step, other, other, other).wait_recv()
        own_copy(step).wait()
        s_high, s_low = halves(recv[step])
        both = jnp.concatenate([s_high, s_low], axis=1)

        def row_tile(j, carry):
            at = pl.multiple_of(j * tile, tile)
            one = jnp.dot(high[pl.ds(at, tile), :], both, preferred_element_type=jnp.float32)
            two = jnp.dot(low[pl.ds(at, tile), :], s_high, preferred_element_type=jnp.float32)
            mixed[step, pl.ds(at, tile), :] = one[:, :piece_width] + (one[:, piece_width:] + two)
            return carry

        lax.fori_loop(0, order // tile, row_tile, 0)
        for d in range(1, band_size):
            back_copy(step, me, lax.rem(me + d, band_size)).start()
        back[step, me] = mixed[step, pl.ds(pl.multiple_of(me * rows, rows), rows), :]

    def turn(i, carry):
        @pl.when(i < channels)
        def _():
            inc_copy(i).wait()

        @pl.when((i < channels) & (window < tm_size - 1))
        def _():
            propagate(i)
            tm_copy(i, window + 1).start()

        @pl.when((i >= LAG) & (i < channels + LAG))
        def _():
            f = i - LAG
            step, part = f // group, lax.rem(f, group)
            sig_copy(f).wait()

            @pl.when(window > 0)
            def _():
                tm_copy(f, window - 1).wait_recv()
                for p in range(pieces):
                    cut = pl.ds(p * piece_width, piece_width)
                    scaled[step, part * pieces + p] = sig[f, :, cut] * (inc[f, :, cut] - arrived[f, :, cut])

            @pl.when(window == 0)
            def _():
                for p in range(pieces):
                    cut = pl.ds(p * piece_width, piece_width)
                    scaled[step, part * pieces + p] = sig[f, :, cut] * inc[f, :, cut]

            for p in range(pieces):
                block = part * pieces + lax.rem(me + p, pieces)

                @pl.when(block != me)
                def _(block=block):
                    block_copy(step, block, me, block).start()

                @pl.when(block == me)
                def _():
                    own_copy(step).start()

        @pl.when(i == LAG)
        def _():
            pass_to_windows()

        @pl.when(i == BACK_LAG - 1)
        def _():
            pass_to_sibling()

        @pl.when(i == BACK_LAG)
        def _():
            split_matrix()

        @pl.when((i >= BACK_LAG) & (lax.rem(i - BACK_LAG + 1, group) == 0))
        def _():
            along_rows((i - BACK_LAG) // group)

        return carry

    lax.fori_loop(0, channels + BACK_LAG, turn, 0)

    contract_last = (((1,), (1,)), ((), ()))

    def along_columns(f, carry):
        step, part = f // group, lax.rem(f, group)
        for p in range(pieces):
            owner = part * pieces + p

            @pl.when(owner != me)
            def _(owner=owner):
                back_copy(step, owner, owner).wait_recv()

        value = jnp.concatenate([back[step, part * pieces + p] for p in range(pieces)], axis=1)
        v_high, v_low = halves(value)
        both = jnp.concatenate([v_high, v_low], axis=0)
        for j in range(width // tile):
            cut = pl.ds(j * tile, tile)
            one = lax.dot_general(both, high[cut, :], contract_last, preferred_element_type=jnp.float32)
            two = lax.dot_general(v_high, low[cut, :], contract_last, preferred_element_type=jnp.float32)
            out[f, :, cut] = sig[f, :, cut] * (one[:rows] + (one[rows:] + two))
        out_copy(f).start()
        return carry

    lax.fori_loop(0, channels, along_columns, 0)

    def sent(step, carry):
        for d in range(1, band_size):
            back_copy(step, me, lax.rem(me + d, band_size)).wait_send()
        return carry

    lax.fori_loop(0, steps, sent, 0)

    def spread_sent(step, carry):
        for d in range(1, band_size):
            other = lax.rem(me + d, band_size)
            block_copy(step, other, me, other).wait_send()
        return carry

    lax.fori_loop(0, steps, spread_sent, 0)

    for h in range(1, pairs):
        share_copy(h, me, onward(h)).wait_send()
        for g in range(1, sharers):
            window_copy(h, g, turn_in, base + lax.rem(turn_in + g, sharers)).wait_send()
    core_copy(0, me).wait_send()
    for h in range(1, pairs):
        core_copy(h, source(h)).wait_send()

    @pl.when(window < tm_size - 1)
    def _():
        def sent(f, carry):
            tm_copy(f, window + 1).wait_send()
            return carry

        lax.fori_loop(0, channels, sent, 0)

    @pl.when(me > 0)
    def _():
        for copy in halo_copies(1, me - 1):
            copy.wait_send()

    @pl.when(me < band_size - 1)
    def _():
        for copy in halo_copies(0, me + 1):
            copy.wait_send()

    def stored(f, carry):
        out_copy(f).wait()
        return carry

    lax.fori_loop(0, channels, stored, 0)


def local(increments, velocity, diffusivity, scaling, correlation):
    band_size, tm_size = lax.axis_size("band"), lax.axis_size("tm")
    rows, width = increments.shape[3:]
    channels = FIELDS * LEVELS
    inc = increments.reshape(channels, rows, width)
    sig = scaling.reshape(channels, rows, width)
    diff = diffusivity.reshape(channels)
    group = max(1, LANES * band_size // width)
    steps = channels // group
    piece_width = width * group // band_size
    order = rows * band_size
    dma = pltpu.SemaphoreType.DMA
    f32 = jnp.float32
    held = pl.BlockSpec(memory_space=pl.ANY)

    sharers = min(tm_size, rows // HALO)
    while tm_size % sharers or rows % (sharers * HALO):
        sharers -= 1
    pairs = band_size // 2

    out = pl.pallas_call(
        functools.partial(defects_kernel, band_size, tm_size, group, sharers),
        out_shape=jax.ShapeDtypeStruct((channels, rows, width), f32),
        in_specs=[held, held, pl.BlockSpec(memory_space=pltpu.SMEM), held, held],
        out_specs=held,
        scratch_shapes=[
            pltpu.VMEM((channels, rows, width), f32),
            pltpu.VMEM((2, rows, width), f32),
            pltpu.VMEM((channels, rows, width), f32),
            pltpu.VMEM((channels, rows, width), f32),
            dma((1,)),
            dma((1,)),
            dma((channels,)),
            dma((channels,)),
            dma((channels,)),
            pltpu.VMEM((order, order), f32),
            pltpu.VMEM((order, order), jnp.bfloat16),
            pltpu.VMEM((order, order), jnp.bfloat16),
            pltpu.VMEM((steps, order, piece_width), f32),
            pltpu.VMEM((steps, band_size, rows, piece_width), f32),
            pltpu.VMEM((steps, order, piece_width), f32),
            pltpu.VMEM((channels, rows, width), f32),
            pltpu.VMEM((channels, rows, width), f32),
            pltpu.VMEM((steps, band_size, rows, piece_width), f32),
            pltpu.VMEM((rows + 4 * HALO, width), f32),
            pltpu.VMEM((rows + 4 * HALO, width), f32),
            pltpu.VMEM((rows + 4 * HALO, width), f32),
            pltpu.VMEM((rows + 4 * HALO, width), f32),
            pltpu.VMEM((2, channels, HALO, width), f32),
            pltpu.VMEM((2, 2, HALO, width), f32),
            dma((2, 2)),
            dma((2, 2)),
            dma((channels,)),
            dma((channels,)),
            dma((steps, band_size)),
            dma((steps, band_size)),
            dma((steps,)),
            dma((steps, band_size)),
            dma((steps, band_size)),
            dma((pairs,)),
            dma((pairs,)),
            dma((pairs, sharers)),
            dma((pairs, sharers)),
            dma((pairs,)),
            dma((pairs,)),
        ],
        compiler_params=pltpu.CompilerParams(
            collective_id=0, has_side_effects=True, vmem_limit_bytes=VMEM_LIMIT
        ),
        cost_estimate=pl.CostEstimate(
            flops=12 * channels * rows * width * order, bytes_accessed=16 * channels * rows * width, transcendentals=0
        ),
        name="defects",
    )(inc, velocity[0], diff, sig, correlation)
    return out.reshape(1, FIELDS, LEVELS, rows, width)


def solution(mesh):
    return jax.shard_map(
        local,
        mesh=mesh,
        in_specs=(
            P("tm", None, None, "band", None),
            P("tm", None, "band", None),
            P(),
            P(None, None, "band", None),
            P("band", None),
        ),
        out_specs=P("tm", None, None, "band", None),
        check_vma=False,
    )
```

```python
import functools

import jax
import jax.numpy as jnp
from jax import lax
from jax.experimental import pallas as pl
from jax.experimental.pallas import tpu as pltpu
from jax.sharding import PartitionSpec as P

FIELDS = 4
LEVELS = 2
STEPS = 4
HALO = 8
LANES = 128
LAG = 2
BACK_LAG = 5
MESH = pl.DeviceIdType.MESH
VMEM_LIMIT = 60 * 1024 * 1024


def greet(band_size, tm_size, sharers):
    me = lax.axis_index("band")
    window = lax.axis_index("tm")
    base = window - lax.rem(window, sharers)
    barrier = pltpu.get_barrier_semaphore()
    for d in range(1, band_size):
        pl.semaphore_signal(
            barrier, inc=1, device_id={"band": lax.rem(me + d, band_size)}, device_id_type=MESH
        )
    for d in range(1, sharers):
        other = base + lax.rem(window - base + d, sharers)
        pl.semaphore_signal(barrier, inc=1, device_id={"tm": other}, device_id_type=MESH)
    before = (window > 0) & (window == base)
    after = (window < tm_size - 1) & (window == base + sharers - 1)

    @pl.when(before)
    def _():
        pl.semaphore_signal(barrier, inc=1, device_id={"tm": window - 1}, device_id_type=MESH)

    @pl.when(after)
    def _():
        pl.semaphore_signal(barrier, inc=1, device_id={"tm": window + 1}, device_id_type=MESH)

    peers = band_size - 1 + sharers - 1 + before.astype(jnp.int32) + after.astype(jnp.int32)
    pl.semaphore_wait(barrier, peers)


def halves(value):
    high = value.astype(jnp.bfloat16)
    return high, (value - high.astype(jnp.float32)).astype(jnp.bfloat16)


def defects_kernel(
    band_size, tm_size, group, sharers,
    inc_in, vel_in, diff, sig_in, corr,
    result,
    inc, vel, sig, out, vel_load, corr_load, inc_load, sig_load, out_store,
    full, high, low, mixed, back, recv, ends, arrived, scaled, ping, pong, east_speed, north_speed, halo_x, halo_v,
    halo_send, halo_recv, tm_send, tm_recv, a2a_send, a2a_recv, own_sem, back_send, back_recv,
    share_send, share_recv, window_send, window_recv, core_send, core_recv,
):
    channels, rows, width = inc_in.shape
    pieces = band_size // group
    piece_width = width // pieces
    steps = channels // group
    me = lax.axis_index("band")
    window = lax.axis_index("tm")

    order = band_size * rows
    half_rows = rows // 2
    part = rows // sharers
    tile = min(order, 512)
    pairs = band_size // 2
    chip, core = me // 2, lax.rem(me, 2)
    sibling = me + 1 - 2 * core
    turn_in = lax.rem(window, sharers)
    base = window - turn_in

    def inc_copy(f):
        return pltpu.make_async_copy(inc_in.at[f], inc.at[f], inc_load.at[f])

    def sig_copy(f):
        return pltpu.make_async_copy(sig_in.at[f], sig.at[f], sig_load.at[f])

    def out_copy(f):
        return pltpu.make_async_copy(out.at[f], result.at[f], out_store.at[f])

    own_rows = pl.ds(pl.multiple_of(me * rows, rows), rows)
    vel_copy = pltpu.make_async_copy(vel_in, vel, vel_load.at[0])
    corr_copy = pltpu.make_async_copy(corr, full.at[own_rows, :], corr_load.at[0])

    vel_copy.start()

    def load(f, carry):
        inc_copy(f).start()
        return carry

    lax.fori_loop(0, channels, load, 0)

    greet(band_size, tm_size, sharers)

    def halo_copies(side, neighbour):
        own = pl.ds(0, HALO) if side else pl.ds(rows - HALO, HALO)
        return [
            pltpu.make_async_remote_copy(
                src_ref=array.at[:, own, :],
                dst_ref=store.at[side],
                send_sem=halo_send.at[side, kind],
                recv_sem=halo_recv.at[side, kind],
                device_id={"band": neighbour},
                device_id_type=MESH,
            )
            for kind, (array, store) in enumerate(((vel_in, halo_v), (inc_in, halo_x)))
        ]

    @pl.when(me > 0)
    def _():
        for copy in halo_copies(1, me - 1):
            copy.start()

    @pl.when(me < band_size - 1)
    def _():
        for copy in halo_copies(0, me + 1):
            copy.start()

    def source(h):
        return 2 * lax.rem(chip - h + pairs, pairs) + core

    def share_rows(band, share):
        return pl.ds(pl.multiple_of(band * rows + share * part, part), part)

    def band_rows(band):
        return pl.ds(pl.multiple_of(band * rows, rows), rows)

    def share_copy(h, owner, other):
        return pltpu.make_async_remote_copy(
            src_ref=corr.at[pl.ds(pl.multiple_of(turn_in * part, part), part), :],
            dst_ref=full.at[share_rows(owner, turn_in), :],
            send_sem=share_send.at[h],
            recv_sem=share_recv.at[h],
            device_id={"band": other},
            device_id_type=MESH,
        )

    def window_copy(h, g, share, other):
        at = share_rows(source(h), share)
        return pltpu.make_async_remote_copy(
            src_ref=full.at[at, :],
            dst_ref=full.at[at, :],
            send_sem=window_send.at[h, g],
            recv_sem=window_recv.at[h, g],
            device_id={"tm": other},
            device_id_type=MESH,
        )

    def core_copy(h, owner):
        at = band_rows(owner)
        return pltpu.make_async_remote_copy(
            src_ref=corr if h == 0 else full.at[at, :],
            dst_ref=full.at[at, :],
            send_sem=core_send.at[h],
            recv_sem=core_recv.at[h],
            device_id={"band": sibling},
            device_id_type=MESH,
        )

    def onward(h):
        return 2 * lax.rem(chip + h, pairs) + core

    for h in range(1, pairs):
        share_copy(h, me, onward(h)).start()
    core_copy(0, me).start()

    def load_scaling(f, carry):
        sig_copy(f).start()
        return carry

    lax.fori_loop(0, channels, load_scaling, 0)
    corr_copy.start()

    def pass_to_windows():
        for h in range(1, pairs):
            share_copy(h, source(h), source(h)).wait_recv()
            for g in range(1, sharers):
                window_copy(h, g, turn_in, base + lax.rem(turn_in + g, sharers)).start()

    def pass_to_sibling():
        for h in range(1, pairs):
            for g in range(1, sharers):
                share = lax.rem(turn_in - g + sharers, sharers)
                window_copy(h, g, share, base + share).wait_recv()
            core_copy(h, source(h)).start()

    def split_matrix():
        corr_copy.wait()
        for h in range(pairs):
            core_copy(h, source(h) + 1 - 2 * core).wait_recv()

        def split(j, carry):
            at = pl.multiple_of(j * 64, 64)
            high[pl.ds(at, 64), :], low[pl.ds(at, 64), :] = halves(full[pl.ds(at, 64), :])
            return carry

        lax.fori_loop(0, order // 64, split, 0)

    zeros = jnp.zeros((HALO, width), jnp.float32)
    for store in (ping, pong):
        store[pl.ds(0, HALO), :] = zeros
        store[pl.ds(rows + 3 * HALO, HALO), :] = zeros

    @pl.when(me == 0)
    def _():
        halo_x[0] = jnp.zeros(halo_x.shape[1:], jnp.float32)
        halo_v[0] = jnp.zeros(halo_v.shape[1:], jnp.float32)

    @pl.when(me == band_size - 1)
    def _():
        halo_x[1] = jnp.zeros(halo_x.shape[1:], jnp.float32)
        halo_v[1] = jnp.zeros(halo_v.shape[1:], jnp.float32)

    def inner_speeds(j, carry):
        at = pl.multiple_of(j * HALO, HALO)
        east_speed[pl.ds(at + 2 * HALO, HALO), :] = 0.5 * vel[0, pl.ds(at, HALO), :]
        north_speed[pl.ds(at + 2 * HALO, HALO), :] = 0.5 * vel[1, pl.ds(at, HALO), :]
        return carry

    vel_copy.wait()
    lax.fori_loop(0, rows // HALO, inner_speeds, 0, unroll=4)

    @pl.when(me > 0)
    def _():
        for copy in halo_copies(0, me - 1):
            copy.wait_recv()

    @pl.when(me < band_size - 1)
    def _():
        for copy in halo_copies(1, me + 1):
            copy.wait_recv()

    for side, at in ((0, HALO), (1, rows + 2 * HALO)):
        east_speed[pl.ds(at, HALO), :] = 0.5 * halo_v[side, 0]
        north_speed[pl.ds(at, HALO), :] = 0.5 * halo_v[side, 1]

    def tangent_step(src, k, first, count, put):
        def strip(j, carry):
            at = pl.multiple_of((first + j) * HALO, HALO)
            near = src[pl.ds(pl.multiple_of(at - HALO, HALO), 3 * HALO), :]
            now = near[HALO : 2 * HALO]
            upper = pltpu.roll(near, 3 * HALO - 1, 0)[HALO : 2 * HALO]
            lower = pltpu.roll(near, 1, 0)[HALO : 2 * HALO]
            eastern = pltpu.roll(now, width - 1, 1)
            western = pltpu.roll(now, 1, 1)
            after = (
                now
                - east_speed[pl.ds(at, HALO), :] * (eastern - western)
                - north_speed[pl.ds(at, HALO), :] * (upper - lower)
                + k * (upper + lower + eastern + western - 4.0 * now)
            )
            place = me * (rows // HALO) + first + j - 2
            inside = (place >= 0) & (place < band_size * (rows // HALO))
            put(at, after * jnp.where(inside, 1.0, 0.0))
            return carry

        unroll = max(n for n in range(1, 7) if count % n == 0)
        lax.fori_loop(0, count, strip, 0, unroll=unroll)

    def propagate(f):
        k = diff[f]

        def fill(j, carry):
            at = pl.multiple_of(j * HALO, HALO)
            ping[pl.ds(at + 2 * HALO, HALO), :] = inc[f, pl.ds(at, HALO), :]
            return carry

        lax.fori_loop(0, rows // HALO, fill, 0, unroll=4)
        ping[pl.ds(HALO, HALO), :] = halo_x[0, f]
        ping[pl.ds(rows + 2 * HALO, HALO), :] = halo_x[1, f]
        stores = (ping, pong)
        for section in range(STEPS - 1):
            target = stores[(section + 1) % 2]

            def put(at, value, target=target):
                target[pl.ds(at, HALO), :] = value

            tangent_step(stores[section % 2], k, 1, rows // HALO + 2, put)

        def put_end(at, value):
            ends[f, pl.ds(pl.multiple_of(at - 2 * HALO, HALO), HALO), :] = value

        tangent_step(stores[(STEPS - 1) % 2], k, 2, rows // HALO, put_end)

    def tm_copy(f, half, other):
        at = pl.ds(half * half_rows, half_rows)
        return pltpu.make_async_remote_copy(
            src_ref=ends.at[f, at, :],
            dst_ref=arrived.at[f, at, :],
            send_sem=tm_send.at[f, half],
            recv_sem=tm_recv.at[f, half],
            device_id={"tm": other},
            device_id_type=MESH,
        )

    def block_copy(step, half, block, owner, other):
        return pltpu.make_async_remote_copy(
            src_ref=scaled.at[step, block, pl.ds(half * half_rows, half_rows), :],
            dst_ref=recv.at[step, pl.ds(pl.multiple_of(owner * rows + half * half_rows, half_rows), half_rows), :],
            send_sem=a2a_send.at[step, half, block],
            recv_sem=a2a_recv.at[step, half, owner],
            device_id={"band": other},
            device_id_type=MESH,
        )

    def own_copy(step):
        return pltpu.make_async_copy(
            scaled.at[step, me],
            recv.at[step, pl.ds(pl.multiple_of(me * rows, rows), rows), :],
            own_sem.at[step],
        )

    def back_copy(step, owner, other):
        return pltpu.make_async_remote_copy(
            src_ref=mixed.at[step, pl.ds(pl.multiple_of(other * rows, rows), rows), :],
            dst_ref=back.at[step, owner],
            send_sem=back_send.at[step, other],
            recv_sem=back_recv.at[step, owner],
            device_id={"band": other},
            device_id_type=MESH,
        )

    def along_rows(step):
        for d in range(1, band_size):
            other = lax.rem(me + d, band_size)
            for half in range(2):
                block_copy(step, half, other, other, other).wait_recv()
        own_copy(step).wait()
        s_high, s_low = halves(recv[step])
        both = jnp.concatenate([s_high, s_low], axis=1)

        def row_tile(j, carry):
            at = pl.multiple_of(j * tile, tile)
            one = jnp.dot(high[pl.ds(at, tile), :], both, preferred_element_type=jnp.float32)
            two = jnp.dot(low[pl.ds(at, tile), :], s_high, preferred_element_type=jnp.float32)
            mixed[step, pl.ds(at, tile), :] = one[:, :piece_width] + (one[:, piece_width:] + two)
            return carry

        lax.fori_loop(0, order // tile, row_tile, 0)
        for d in range(1, band_size):
            back_copy(step, me, lax.rem(me + d, band_size)).start()
        back[step, me] = mixed[step, pl.ds(pl.multiple_of(me * rows, rows), rows), :]

    def turn(i, carry):
        @pl.when(i < channels)
        def _():
            inc_copy(i).wait()

        @pl.when((i < channels) & (window < tm_size - 1))
        def _():
            propagate(i)
            for half in range(2):
                tm_copy(i, half, window + 1).start()

        @pl.when((i >= LAG) & (i < channels + LAG))
        def _():
            f = i - LAG
            step, part = f // group, lax.rem(f, group)
            sig_copy(f).wait()

            for half in range(2):
                at = pl.ds(half * half_rows, half_rows)

                @pl.when(window > 0)
                def _(half=half, at=at):
                    tm_copy(f, half, window - 1).wait_recv()
                    for p in range(pieces):
                        cut = pl.ds(p * piece_width, piece_width)
                        scaled[step, part * pieces + p, at, :] = sig[f, at, cut] * (
                            inc[f, at, cut] - arrived[f, at, cut]
                        )

                @pl.when(window == 0)
                def _(at=at):
                    for p in range(pieces):
                        cut = pl.ds(p * piece_width, piece_width)
                        scaled[step, part * pieces + p, at, :] = sig[f, at, cut] * inc[f, at, cut]

                for p in range(pieces):
                    block = part * pieces + lax.rem(me + p, pieces)

                    @pl.when(block != me)
                    def _(block=block, half=half):
                        block_copy(step, half, block, me, block).start()

            @pl.when(me // pieces == part)
            def _():
                own_copy(step).start()

        @pl.when(i == LAG)
        def _():
            pass_to_windows()

        @pl.when(i == BACK_LAG - 1)
        def _():
            pass_to_sibling()

        @pl.when(i == BACK_LAG)
        def _():
            split_matrix()

        @pl.when((i >= BACK_LAG) & (lax.rem(i - BACK_LAG + 1, group) == 0))
        def _():
            along_rows((i - BACK_LAG) // group)

        return carry

    lax.fori_loop(0, channels + BACK_LAG, turn, 0)

    contract_last = (((1,), (1,)), ((), ()))

    def along_columns(f, carry):
        step, part = f // group, lax.rem(f, group)
        for p in range(pieces):
            owner = part * pieces + p

            @pl.when(owner != me)
            def _(owner=owner):
                back_copy(step, owner, owner).wait_recv()

        value = jnp.concatenate([back[step, part * pieces + p] for p in range(pieces)], axis=1)
        v_high, v_low = halves(value)
        both = jnp.concatenate([v_high, v_low], axis=0)
        for j in range(width // tile):
            cut = pl.ds(j * tile, tile)
            one = lax.dot_general(both, high[cut, :], contract_last, preferred_element_type=jnp.float32)
            two = lax.dot_general(v_high, low[cut, :], contract_last, preferred_element_type=jnp.float32)
            out[f, :, cut] = sig[f, :, cut] * (one[:rows] + (one[rows:] + two))
        out_copy(f).start()
        return carry

    lax.fori_loop(0, channels, along_columns, 0)

    def sent(step, carry):
        for d in range(1, band_size):
            back_copy(step, me, lax.rem(me + d, band_size)).wait_send()
        return carry

    lax.fori_loop(0, steps, sent, 0)

    def spread_sent(step, carry):
        for d in range(1, band_size):
            other = lax.rem(me + d, band_size)
            for half in range(2):
                block_copy(step, half, other, me, other).wait_send()
        return carry

    lax.fori_loop(0, steps, spread_sent, 0)

    for h in range(1, pairs):
        share_copy(h, me, onward(h)).wait_send()
        for g in range(1, sharers):
            window_copy(h, g, turn_in, base + lax.rem(turn_in + g, sharers)).wait_send()
    core_copy(0, me).wait_send()
    for h in range(1, pairs):
        core_copy(h, source(h)).wait_send()

    @pl.when(window < tm_size - 1)
    def _():
        def sent(f, carry):
            for half in range(2):
                tm_copy(f, half, window + 1).wait_send()
            return carry

        lax.fori_loop(0, channels, sent, 0)

    @pl.when(me > 0)
    def _():
        for copy in halo_copies(1, me - 1):
            copy.wait_send()

    @pl.when(me < band_size - 1)
    def _():
        for copy in halo_copies(0, me + 1):
            copy.wait_send()

    def stored(f, carry):
        out_copy(f).wait()
        return carry

    lax.fori_loop(0, channels, stored, 0)


def local(increments, velocity, diffusivity, scaling, correlation):
    band_size, tm_size = lax.axis_size("band"), lax.axis_size("tm")
    rows, width = increments.shape[3:]
    channels = FIELDS * LEVELS
    inc = increments.reshape(channels, rows, width)
    sig = scaling.reshape(channels, rows, width)
    diff = diffusivity.reshape(channels)
    group = max(1, LANES * band_size // width)
    steps = channels // group
    piece_width = width * group // band_size
    order = rows * band_size
    dma = pltpu.SemaphoreType.DMA
    f32 = jnp.float32
    held = pl.BlockSpec(memory_space=pl.ANY)

    sharers = min(tm_size, rows // HALO)
    while tm_size % sharers or rows % (sharers * HALO):
        sharers -= 1
    pairs = band_size // 2

    out = pl.pallas_call(
        functools.partial(defects_kernel, band_size, tm_size, group, sharers),
        out_shape=jax.ShapeDtypeStruct((channels, rows, width), f32),
        in_specs=[held, held, pl.BlockSpec(memory_space=pltpu.SMEM), held, held],
        out_specs=held,
        scratch_shapes=[
            pltpu.VMEM((channels, rows, width), f32),
            pltpu.VMEM((2, rows, width), f32),
            pltpu.VMEM((channels, rows, width), f32),
            pltpu.VMEM((channels, rows, width), f32),
            dma((1,)),
            dma((1,)),
            dma((channels,)),
            dma((channels,)),
            dma((channels,)),
            pltpu.VMEM((order, order), f32),
            pltpu.VMEM((order, order), jnp.bfloat16),
            pltpu.VMEM((order, order), jnp.bfloat16),
            pltpu.VMEM((steps, order, piece_width), f32),
            pltpu.VMEM((steps, band_size, rows, piece_width), f32),
            pltpu.VMEM((steps, order, piece_width), f32),
            pltpu.VMEM((channels, rows, width), f32),
            pltpu.VMEM((channels, rows, width), f32),
            pltpu.VMEM((steps, band_size, rows, piece_width), f32),
            pltpu.VMEM((rows + 4 * HALO, width), f32),
            pltpu.VMEM((rows + 4 * HALO, width), f32),
            pltpu.VMEM((rows + 4 * HALO, width), f32),
            pltpu.VMEM((rows + 4 * HALO, width), f32),
            pltpu.VMEM((2, channels, HALO, width), f32),
            pltpu.VMEM((2, 2, HALO, width), f32),
            dma((2, 2)),
            dma((2, 2)),
            dma((channels, 2)),
            dma((channels, 2)),
            dma((steps, 2, band_size)),
            dma((steps, 2, band_size)),
            dma((steps,)),
            dma((steps, band_size)),
            dma((steps, band_size)),
            dma((pairs,)),
            dma((pairs,)),
            dma((pairs, sharers)),
            dma((pairs, sharers)),
            dma((pairs,)),
            dma((pairs,)),
        ],
        compiler_params=pltpu.CompilerParams(
            collective_id=0, has_side_effects=True, vmem_limit_bytes=VMEM_LIMIT
        ),
        cost_estimate=pl.CostEstimate(
            flops=12 * channels * rows * width * order, bytes_accessed=16 * channels * rows * width, transcendentals=0
        ),
        name="defects",
    )(inc, velocity[0], diff, sig, correlation)
    return out.reshape(1, FIELDS, LEVELS, rows, width)


def solution(mesh):
    return jax.shard_map(
        local,
        mesh=mesh,
        in_specs=(
            P("tm", None, None, "band", None),
            P("tm", None, "band", None),
            P(),
            P(None, None, "band", None),
            P("band", None),
        ),
        out_specs=P("tm", None, None, "band", None),
        check_vma=False,
    )
```
